32 devices in a mesh: batch: 4 (over y, x), mp: 8 (over z, core).
Axes of the slice: x: 2, y: 2, z: 4, core: 2. Of those that a mesh axis runs over, the one named last changes fastest.
Arguments:
- pool_in: bfloat16 [2, 2048, 9216], P(None, 'batch', 'mp'), may hold values from -6 to 6
- weights: bfloat16 [2, 9216, 4096], P(None, None, 'mp'), may hold values from -0.0625 to 0.0625
- bias: float32 [2, 4096], P(None, 'mp'), may hold values from -3 to 3
- stitch: float32 [2, 2, 4096], P(None, None, 'mp')
- crops: int32 [512], P('batch'), may hold values from 1 to 4, as said below
- row_mask: int32 [2048], P('batch'), may hold values 0 or 1
- cotangent: bfloat16 [2, 2048, 4096], P(None, 'batch', 'mp'), may hold values from -6 to 6
Outputs:
- mixed: bfloat16 [2, 2048, 4096], P(None, 'batch')
- input_grad: bfloat16 [2, 2048, 9216], P(None, 'batch', 'mp')
- weight_grad: float32 [2, 9216, 4096], P(None, None, 'mp')
- bias_grad: float32 [2, 4096], P(None, 'mp')
- stitch_grad: float32 [2, 2, 4096], P(None, None, 'mp')
The draws below stay inside these ranges and needn't reach their ends.
Inputs may be any that keep to these rules, and one draw needn't show every extreme that they name: crops of the images of each batch shard; every shard has an image of one crop.
All inputs are finite; a program needn't handle non-finite values. No bound on the sum of `row_mask` on one device may be relied on, other than what follows from the above.
Results may differ from the reference program's by a relative error of at most 0.005.
Values may be sent and summed in bfloat16 or wider, within the bound.
A program may use at most 320 MiB of HBM per device.

```python
import jax
import jax.numpy as jnp
from jax import lax

D_IN = 9216
D_OUT = 4096
TASKS = 2
IMG_DEV = 128
ROWS_DEV = 512
IMAGES = 512
ROWS = 2048


def draw_stitch(key, part):
    key = jax.random.fold_in(key, 11)
    base = jax.random.uniform(key, (TASKS, TASKS, D_OUT), jnp.float32)
    eye = jnp.eye(TASKS, dtype=jnp.float32)[:, :, None]
    return eye * (0.6 + 0.4 * base) + (1.0 - eye) * (0.2 + 0.3 * base)


def draw_crops(key, part):
    key = jax.random.fold_in(key, 23)
    first, second = jax.random.split(key)
    shards = IMAGES // IMG_DEV
    caps = jax.random.randint(first, (shards,), 1, 5)
    caps = caps.at[0].set(4)
    raw = jax.random.randint(second, (shards, IMG_DEV), 0, 1 << 20)
    counts = raw % caps[:, None] + 1
    counts = counts.at[0, 0].set(4)
    counts = counts.at[:, 1].set(1)
    return counts.reshape(-1).astype(jnp.int32)


def with_ends(drawn, own_key, least, largest):
    dims = drawn.shape
    spot = [jax.random.randint(jax.random.fold_in(own_key, axis), (), 0, dims[axis]) for axis in range(len(dims))]
    drawn = drawn.at[tuple(spot)].set(least)
    longest = dims.index(max(dims))
    spot[longest] = (spot[longest] + 1) % dims[longest]
    return drawn.at[tuple(spot)].set(largest)


def level_of(own_key, dims, cuts, smallest, largest):
    gain = 1.0
    for axis_at, blocks in cuts:
        steps = jax.random.uniform(jax.random.fold_in(jax.random.fold_in(own_key, 6), axis_at), (blocks,), jnp.float32, smallest / len(cuts), largest / len(cuts))
        gain = gain * jnp.repeat(jnp.exp(steps), dims[axis_at] // blocks).reshape((-1,) + (1,) * (len(dims) - 1 - axis_at))
    return gain


def noise(own_key, shape, spread, limit, cuts=(), kind=jnp.bfloat16):
    factor_of = level_of(own_key, shape, cuts, -0.22, 0.18) if cuts else 1.0
    result = jax.random.normal(own_key, shape, jnp.float32) * spread * factor_of
    return jnp.minimum(jnp.maximum(result, -limit), limit).astype(kind)


def setup_inputs(seed: int = 0) -> dict:
    key_list = jax.random.split(jax.random.key(seed), 8)
    return {
        "pool_in": noise(key_list[0], (TASKS, ROWS, D_IN), 1.0, 6.0, ((1, 4), (2, 8))),
        "weights": noise(key_list[1], (TASKS, D_IN, D_OUT), D_IN ** -0.5, 0.0625, ((2, 8),)),
        "bias": noise(key_list[2], (TASKS, D_OUT), 0.5, 3.0, ((1, 8),), jnp.float32),
        "stitch": draw_stitch(jax.random.fold_in(key_list[7], 71), 0),
        "crops": draw_crops(jax.random.fold_in(key_list[7], 71), 0),
        "row_mask": with_ends((jax.random.randint(key_list[5], (ROWS,), 0, 4) < 3).astype(jnp.int32), jax.random.fold_in(key_list[5], 1), 0, 1),
        "cotangent": noise(key_list[6], (TASKS, ROWS, D_OUT), 1.0, 6.0, ((1, 4), (2, 8))),
    }


@jax.custom_vjp
def low(v):
    return lax.optimization_barrier(v.astype(jnp.bfloat16)).astype(jnp.float32)

@jax.custom_vjp
def low_back(v):
    return v

def low_keep(v):
    return (low(v), None)

def low_pass(kept, grad):
    return (grad,)

def back_keep(v):
    return (v, None)

def back_low(kept, grad):
    return (low(grad),)
low.defvjp(low_keep, low_pass)
low_back.defvjp(back_keep, back_low)

def row_weights(crops, row_mask):
    shards = IMAGES // IMG_DEV
    counts = crops.reshape(shards, IMG_DEV)
    ends = jnp.cumsum(counts, axis=1)
    slots = jnp.arange(ROWS_DEV, dtype=jnp.int32)
    image = lax.optimization_barrier(jnp.sum((slots[None, :, None] >= ends[:, None, :]).astype(jnp.int32), axis=2))
    inside = slots[None, :] < ends[:, -1:]
    onehot = (image[:, :, None] == jnp.arange(IMG_DEV, dtype=jnp.int32)[None, None, :]).astype(jnp.int32)
    count = lax.optimization_barrier(jnp.sum(onehot * counts[:, None, :], axis=2))
    count = jnp.where(inside, count, 1).astype(jnp.float32).reshape(-1)
    valid = (row_mask.reshape(shards, ROWS_DEV) * inside.astype(jnp.int32)).astype(jnp.float32).reshape(-1)
    return (count, valid)

def reference(pool_in, weights, bias, stitch, crops, row_mask, cotangent):
    count, valid = row_weights(crops, row_mask)
    hp = lax.Precision.HIGHEST

    def forward(inputs, mats, offsets, units):
        pre = jnp.einsum('trk,tkc->trc', inputs, mats, precision=hp) + offsets[:, None, :]
        pre = low_back(pre)
        hidden = jax.nn.gelu(pre)
        stitched = jnp.einsum('tuc,urc->trc', units, hidden, precision=hp)
        return low(valid[None, :, None] * stitched)
    primal = (pool_in.astype(jnp.float32), weights.astype(jnp.float32), bias, stitch)
    out, pullback = jax.vjp(forward, *primal)
    scaled = cotangent.astype(jnp.float32) / count[None, :, None]
    d_in, d_w, d_b, d_s = pullback(scaled)
    return (out.astype(jnp.bfloat16), d_in.astype(jnp.bfloat16), d_w, d_b, d_s)
```

```python
import functools

import jax
import jax.numpy as jnp
from jax import lax
from jax.experimental import pallas as pl
from jax.experimental.pallas import tpu as pltpu
from jax.sharding import PartitionSpec as P

MESH = pl.DeviceIdType.MESH
F32 = jnp.float32
BF16 = jnp.bfloat16
LAYERS = 4
GROUP = 4
TASKS = 2
TANH_SCALE = 0.7978845608
TANH_CUBE = 0.044715


def row_weights(crops, row_mask):
    slots = jnp.arange(row_mask.shape[0], dtype=jnp.int32)
    ends = jnp.cumsum(crops)
    image = jnp.sum((slots[:, None] >= ends[None, :]).astype(jnp.int32), axis=1)
    inside = slots < ends[-1]
    onehot = (image[:, None] == jnp.arange(crops.shape[0], dtype=jnp.int32)[None, :]).astype(
        jnp.int32
    )
    count = jnp.sum(onehot * crops[None, :], axis=1)
    count = jnp.where(inside, count, 1).astype(jnp.float32)
    valid = (row_mask * inside.astype(jnp.int32)).astype(jnp.float32)
    return (count, valid)


def exchange(xc, w, bias, stitch, cot, scale, kept, xg, dg, mg, ig, st,
             wv, pre, dpv, mxv, xbuf, acc, sbuf, rup, rdn, tso, tsi, stv,
             wsem, lsem, osem, z_r, z_u, z_d, o_x, o_y, r_x, r_y, r_d, f_s, c_r, c_s,
             dp_s, dp_r, m_r, m_u, m_d, mc_r, mc_s, t_u, t_d, t_s, tc_r, tc_s, st_s, st_r, ig_s):
    rows, depth = xc.shape[1], xc.shape[2]
    cols = w.shape[2]
    b, m = lax.axis_index("batch"), lax.axis_index("mp")
    z, c = m // 2, m % 2
    y, x = b // 2, b % 2
    bx, by, bd = y * 2 + (1 - x), (1 - y) * 2 + x, 3 - b
    to_x, to_y, to_d = (bx, m), (by, m), (bd, m)
    to_c = (b, z * 2 + 1 - c)
    up, down = (b, m + 2), (b, m - 2)
    not_top, not_bottom = z < LAYERS - 1, z > 0
    everyone = [(None, to_x), (None, to_y), (None, to_d), (None, to_c), (not_top, up), (not_bottom, down)]

    barrier = pltpu.get_barrier_semaphore()
    for cond, dev in everyone:
        def greet(dev=dev):
            pl.semaphore_signal(barrier, inc=1, device_id=dev, device_id_type=MESH)
        greet() if cond is None else pl.when(cond)(greet)
    ends = LAYERS - 1
    pl.semaphore_wait(barrier, 4 + (z + ends - 1) // ends + (2 * ends - 1 - z) // ends)

    drains = []

    def remote(src, dst, send, recv, dev):
        return pltpu.make_async_remote_copy(
            src_ref=src, dst_ref=dst, send_sem=send, recv_sem=recv, device_id=dev, device_id_type=MESH)

    def send(src, dst, ssem, rsem, dev, cond=None):
        def go():
            remote(src, dst, ssem, rsem, dev).start()
        def drain():
            remote(src, dst, ssem, rsem, dev).wait_send()
        if cond is None:
            go()
            drains.append(drain)
        else:
            pl.when(cond)(go)
            drains.append(lambda: pl.when(cond)(drain))

    def arrived(dst, rsem, cond=None):
        def go():
            remote(dst, dst, rsem, rsem, to_c).wait_recv()
        go() if cond is None else pl.when(cond)(go)

    def local(src, dst, sem):
        copy = pltpu.make_async_copy(src, dst, sem)
        copy.start()
        drains.append(copy.wait)
        return copy

    def span(who):
        return pl.ds(pl.multiple_of(who * rows, 16), rows)

    def slot(t, layer, plane, who):
        return xg.at[layer * 2 + plane, t, span(who), :]

    load_w = pltpu.make_async_copy(w, wv, wsem)
    load_w.start()
    own = [pltpu.make_async_copy(xc.at[t], slot(t, z, c, b), osem.at[t]) for t in range(TASKS)]

    def own_z(t):
        send(xc.at[t], slot(t, z, c, b), z_u.at[t, z], z_r.at[t, z], up, not_top)
        send(xc.at[t], slot(t, z, c, b), z_d.at[t, z], z_r.at[t, z], down, not_bottom)

    def to_square(t, src, layer, cond=None):
        send(src, slot(t, layer, c, b), c_s.at[0, t, layer], c_r.at[0, t, layer], to_c, cond)
        send(src, slot(t, layer, c, b), o_x.at[t, layer], r_x.at[t, layer], to_x, cond)
        send(src, slot(t, layer, c, b), o_y.at[t, layer], r_y.at[t, layer], to_y, cond)

    def z_step(t, d):
        low, high = z - d, z + d
        here = slot(t, low, c, b)
        arrived(here, z_r.at[t, low], z >= d)
        send(here, here, z_u.at[t, low], z_r.at[t, low], up, (z >= d) & not_top)
        to_square(t, here, low, z >= d)
        there = slot(t, high, c, b)
        arrived(there, z_r.at[t, high], z < LAYERS - d)
        send(there, there, z_d.at[t, high], z_r.at[t, high], down, (z < LAYERS - d) & not_bottom)
        to_square(t, there, high, z < LAYERS - d)

    def square_step(t, layer):
        from_x, from_y = slot(t, layer, c, bx), slot(t, layer, c, by)
        arrived(from_x, r_x.at[t, layer])
        if (t + layer) % 2 == 0:
            send(from_x, from_x, f_s.at[t, layer], r_d.at[t, layer], to_y)
        send(from_x, from_x, c_s.at[1, t, layer], c_r.at[1, t, layer], to_c)
        arrived(from_y, r_y.at[t, layer])
        if (t + layer) % 2 == 1:
            send(from_y, from_y, f_s.at[t, layer], r_d.at[t, layer], to_x)
        send(from_y, from_y, c_s.at[2, t, layer], c_r.at[2, t, layer], to_c)

    def corner_step(t, layer):
        from_d = slot(t, layer, c, bd)
        arrived(from_d, r_d.at[t, layer])
        send(from_d, from_d, c_s.at[3, t, layer], c_r.at[3, t, layer], to_c)

    def forward(t):
        for layer in range(LAYERS):
            arrived(slot(t, layer, 1 - c, b), c_r.at[0, t, layer])

        def load(mm, k):
            return pltpu.make_async_copy(xg.at[mm, t, span(b), :], xbuf.at[k], lsem.at[k])

        load(0, 0).start()
        pre[t] = jnp.broadcast_to(bias[t:t + 1, :], (rows, cols))

        def step(mm, carry):
            k = mm % 2
            pl.when(mm + 1 < 2 * LAYERS)(lambda: load(mm + 1, 1 - k).start())
            load(mm, k).wait()
            part = pl.ds(pl.multiple_of(mm * depth, 128), depth)
            for h in range(2):
                half = slice(h * (cols // 2), (h + 1) * (cols // 2))
                pre[t, :, half] += jnp.dot(xbuf[k], wv[t, part, half], preferred_element_type=F32)
            return carry

        lax.fori_loop(0, 2 * LAYERS, step, 0)

    def fold(v):
        return jnp.sum(v.reshape(2, 8, v.shape[1]), axis=0)

    def activate(u):
        def chunk(i, sums):
            s0, s1, bb = sums
            part = pl.ds(pl.multiple_of(i * 16, 16), 16)
            v = pre[u, part, :]
            th = jnp.tanh(TANH_SCALE * (v + TANH_CUBE * (v * v * v)))
            h = 0.5 * v * (1.0 + th)
            slope = 0.5 * (1.0 + th) + 0.5 * v * (1.0 - th * th) * (TANH_SCALE * (1.0 + 3.0 * TANH_CUBE * (v * v)))
            sc = scale[part, :]
            g0 = cot[0, part, :].astype(F32) * sc
            g1 = cot[1, part, :].astype(F32) * sc
            dpre = (slope * (stitch[u:u + 1, :] * g0 + stitch[2 + u:3 + u, :] * g1)).astype(BF16)
            dpv[u, part, :] = dpre
            if u == 0:
                pre[0, part, :] = h
            else:
                h0 = pre[0, part, :]
                for t in range(TASKS):
                    mxv[t, part, :] = (stitch[2 * t:2 * t + 1, :] * h0 + stitch[2 * t + 1:2 * t + 2, :] * h).astype(BF16)
            return s0 + fold(g0 * h), s1 + fold(g1 * h), bb + fold(dpre.astype(F32))

        zero = jnp.zeros((8, cols), F32)
        s0, s1, bb = lax.fori_loop(0, rows // 16, chunk, (zero, zero, zero))
        stv[b, u:u + 1, :] = jnp.sum(s0, axis=0, keepdims=True)
        stv[b, 2 + u:3 + u, :] = jnp.sum(s1, axis=0, keepdims=True)
        stv[b, 4 + u:5 + u, :] = jnp.sum(bb, axis=0, keepdims=True)

    def spread_dpre(t):
        mine = dg.at[t, span(b), :]
        local(dpv.at[t], mine, dp_s.at[t, 3])
        send(dpv.at[t], mine, dp_s.at[t, 0], dp_r.at[t, 0], to_x)
        send(dpv.at[t], mine, dp_s.at[t, 1], dp_r.at[t, 1], to_y)

    def forward_dpre(t):
        from_x, from_y = dg.at[t, span(bx), :], dg.at[t, span(by), :]
        arrived(from_x, dp_r.at[t, 0])
        arrived(from_y, dp_r.at[t, 1])
        if t == 0:
            send(from_x, from_x, dp_s.at[t, 2], dp_r.at[t, 2], to_y)
        else:
            send(from_y, from_y, dp_s.at[t, 2], dp_r.at[t, 2], to_x)

    def own_mixed():
        local(mxv, mg.at[m], mc_s.at[LAYERS])
        send(mxv, mg.at[m], m_u.at[z], m_r.at[z], up, not_top)
        send(mxv, mg.at[m], m_d.at[z], m_r.at[z], down, not_bottom)
        send(mxv, mg.at[m], mc_s.at[z], mc_r.at[z], to_c)

    def mixed_step(d):
        low, high = z - d, z + d
        here = mg.at[low * 2 + c]
        arrived(here, m_r.at[low], z >= d)
        send(here, here, m_u.at[low], m_r.at[low], up, (z >= d) & not_top)
        send(here, here, mc_s.at[low], mc_r.at[low], to_c, z >= d)
        there = mg.at[high * 2 + c]
        arrived(there, m_r.at[high], z < LAYERS - d)
        send(there, there, m_d.at[high], m_r.at[high], down, (z < LAYERS - d) & not_bottom)
        send(there, there, mc_s.at[high], mc_r.at[high], to_c, z < LAYERS - d)

    tiles = 3
    width = depth // tiles

    def term(t, mm, j):
        part = pl.ds(pl.multiple_of(mm * depth + j * width, 128), width)
        return lax.dot_general(dpv[t], wv[t, part, :], (((1,), (1,)), ((), ())), preferred_element_type=F32)

    def core_terms(t):
        def step(s, carry):
            for j in range(tiles):
                tso[t, s, :, j * width:(j + 1) * width] = term(t, 2 * s + 1 - c, j).astype(BF16)
            remote(tso.at[t, s], tsi.at[t, s], tc_s.at[t, s], tc_r.at[t, s], to_c).start()
            return carry

        lax.fori_loop(0, LAYERS, step, 0)
        for s in range(LAYERS):
            drains.append(lambda s=s: remote(
                tso.at[t, s], tsi.at[t, s], tc_s.at[t, s], tc_r.at[t, s], to_c).wait_send())

    def chain_step(t, k):
        s = [3 * (1 - z // 2), (2 + 3 * z) % 5, 1 + z % 2, z][k]
        has_up = (s >= z) & not_bottom
        has_down = (s <= z) & not_top
        arrived(tsi.at[t, s], tc_r.at[t, s])
        arrived(rup.at[t, s], t_u.at[t, s], has_up)
        arrived(rdn.at[t, s], t_d.at[t, s], has_down)
        for j in range(tiles):
            part = slice(j * width, (j + 1) * width)
            acc[...] = term(t, 2 * s + c, j) + tsi[t, s, :, part].astype(F32)

            @pl.when(has_up)
            def _():
                acc[...] += rup[t, s, :, part].astype(F32)

            @pl.when(has_down)
            def _():
                acc[...] += rdn[t, s, :, part].astype(F32)

            sbuf[t, s, :, part] = acc[...].astype(BF16)
        if k < LAYERS - 1:
            send(sbuf.at[t, s], rup.at[t, s], t_s.at[t, s], t_u.at[t, s], up, s > z)
            send(sbuf.at[t, s], rdn.at[t, s], t_s.at[t, s], t_d.at[t, s], down, s < z)
        else:
            local(sbuf.at[t, s], ig.at[t], ig_s.at[t])

    own_z(0)
    to_square(0, xc.at[0], z)
    for copy in own:
        copy.start()
    z_step(0, 1)
    z_step(0, 2)
    own_z(1)
    to_square(1, xc.at[1], z)
    z_step(0, 3)
    for copy in own:
        copy.wait()
    load_w.wait()
    forward(0)
    activate(0)
    spread_dpre(0)
    core_terms(0)
    for i in range(3):
        z_step(1, i + 1)
        chain_step(0, i)
    chain_step(0, 3)
    forward(1)
    activate(1)
    own_mixed()
    spread_dpre(1)
    stv[b, 6:7, :] = kept[...]
    stv[b, 7:8, :] = jnp.zeros((1, cols), F32)
    send(stv.at[b], stv.at[b], st_s.at[0], st_r.at[0], to_x)
    send(stv.at[b], stv.at[b], st_s.at[1], st_r.at[1], to_y)
    send(stv.at[b], stv.at[b], st_s.at[2], st_r.at[2], to_d)
    core_terms(1)
    for i in range(3):
        mixed_step(i + 1)
        chain_step(1, i)
        square_step(0, i)
    chain_step(1, 3)
    square_step(0, 3)
    forward_dpre(0)
    for layer in range(LAYERS):
        square_step(1, layer)
    forward_dpre(1)
    for t in range(TASKS):
        for layer in range(LAYERS):
            corner_step(t, layer)
    for t in range(TASKS):
        arrived(dg.at[t, span(bd), :], dp_r.at[t, 2])
        for layer in range(LAYERS):
            for k, who in ((1, bx), (2, by), (3, bd)):
                arrived(slot(t, layer, 1 - c, who), c_r.at[k, t, layer])
    for layer in range(LAYERS):
        arrived(mg.at[layer * 2 + 1 - c], mc_r.at[layer])
    arrived(stv.at[bx], st_r.at[0])
    arrived(stv.at[by], st_r.at[1])
    arrived(stv.at[bd], st_r.at[2])
    for drain in drains:
        drain()
    st[...] = stv[...]


def run_exchange(xc, weights, bias, stitch, cot, scale, kept):
    tasks, rows, depth = xc.shape
    cols = weights.shape[2]
    parts = weights.shape[1] // depth
    sem = pltpu.SemaphoreType.DMA
    any_spec = pl.BlockSpec(memory_space=pl.ANY)
    vmem_spec = pl.BlockSpec(memory_space=pltpu.VMEM)
    two, four = TASKS, LAYERS
    return pl.pallas_call(
        exchange,
        out_shape=(
            jax.ShapeDtypeStruct((parts, tasks, GROUP * rows, depth), BF16),
            jax.ShapeDtypeStruct((tasks, GROUP * rows, cols), BF16),
            jax.ShapeDtypeStruct((parts, tasks, rows, cols), BF16),
            jax.ShapeDtypeStruct((tasks, rows, depth), BF16),
            jax.ShapeDtypeStruct((GROUP, 8, cols), F32),
        ),
        in_specs=[any_spec, any_spec] + [vmem_spec] * 5,
        out_specs=(any_spec, any_spec, any_spec, any_spec, vmem_spec),
        scratch_shapes=[
            pltpu.VMEM(weights.shape, BF16),
            pltpu.VMEM((tasks, rows, cols), F32),
            pltpu.VMEM((tasks, rows, cols), BF16),
            pltpu.VMEM((tasks, rows, cols), BF16),
            pltpu.VMEM((2, rows, depth), BF16),
            pltpu.VMEM((rows, depth // 3), F32),
            pltpu.VMEM((tasks, LAYERS, rows, depth), BF16),
            pltpu.VMEM((tasks, LAYERS, rows, depth), BF16),
            pltpu.VMEM((tasks, LAYERS, rows, depth), BF16),
            pltpu.VMEM((tasks, LAYERS, rows, depth), BF16),
            pltpu.VMEM((tasks, LAYERS, rows, depth), BF16),
            pltpu.VMEM((GROUP, 8, cols), F32),
            sem, sem((2,)), sem((two,)),
            sem((two, four)), sem((two, four)), sem((two, four)),
            sem((two, four)), sem((two, four)), sem((two, four)), sem((two, four)), sem((two, four)),
            sem((two, four)), sem((4, two, four)), sem((4, two, four)),
            sem((two, 4)), sem((two, 3)),
            sem((four,)), sem((four,)), sem((four,)), sem((four,)), sem((four + 1,)),
            sem((two, four)), sem((two, four)), sem((two, four)), sem((two, four)), sem((two, four)),
            sem((3,)), sem((3,)), sem((two,)),
        ],
        compiler_params=pltpu.CompilerParams(
            collective_id=0, has_side_effects=True, vmem_limit_bytes=60 * 1024 * 1024),
        cost_estimate=pl.CostEstimate(
            flops=4 * tasks * rows * parts * depth * cols, bytes_accessed=80_000_000, transcendentals=0),
    )(xc, weights, bias, stitch, cot, scale, kept)


def packed_body(pool_in, weights, bias, stitch, crops, row_mask, cotangent):
    slots = row_mask.shape[0]
    cols = weights.shape[2]
    rows = (slots * 17 // 32 + 15) // 16 * 16
    count, valid = row_weights(crops, row_mask)
    place = jnp.cumsum(valid.astype(jnp.int32)) - 1
    kept = jnp.sum(valid)
    units = stitch.reshape(TASKS * TASKS, cols)

    def pack(first):
        pick = (place[None, :] == first + jnp.arange(rows, dtype=jnp.int32)[:, None]) & (valid[None, :] > 0)
        pick16 = pick.astype(BF16)
        scale = jnp.sum(pick.astype(F32) * (valid / count)[None, :], axis=1, keepdims=True)
        xc = jnp.einsum("ri,tik->trk", pick16, pool_in, preferred_element_type=F32).astype(BF16)
        cot = jnp.einsum("ri,tik->trk", pick16, cotangent, preferred_element_type=F32).astype(BF16)
        return pick16, run_exchange(xc, weights, bias, units, cot, scale, jnp.full((1, cols), kept, F32))

    def results(passes):
        mixed = sum(jnp.einsum("ri,mtrc->timc", pick, out[2], preferred_element_type=F32) for pick, out in passes)
        mixed = mixed.reshape(TASKS, slots, -1).astype(BF16)
        input_grad = sum(jnp.einsum("ri,trk->tik", pick, out[3], preferred_element_type=F32) for pick, out in passes)
        weight_grad = sum(jnp.einsum("mtrk,trc->tmkc", out[0], out[1], preferred_element_type=F32) for _, out in passes)
        small = sum(jnp.sum(out[4], axis=0) for _, out in passes)
        return (
            mixed,
            input_grad.astype(BF16),
            weight_grad.reshape(weights.shape),
            small[4:6],
            small[0:4].reshape(TASKS, TASKS, cols),
        )

    first = pack(0)
    most = jnp.max(first[1][4][:, 6, 0])
    return lax.cond(most > rows, lambda: results([first, pack(rows)]), lambda: results([first]))


def plain_body(pool_in, weights, bias, stitch, crops, row_mask, cotangent):
    hp = lax.Precision.HIGHEST
    count, valid = row_weights(crops, row_mask)
    features = lax.all_gather(pool_in, "mp", axis=2, tiled=True)
    linear = jnp.einsum("trk,tkc->trc", features, weights, preferred_element_type=jnp.float32)
    pre = linear + bias[:, None, :]
    hidden, gelu_back = jax.vjp(jax.nn.gelu, pre)
    stitched = stitch[:, 0, None, :] * hidden[0][None] + stitch[:, 1, None, :] * hidden[1][None]
    local_mixed = (valid[None, :, None] * stitched).astype(jnp.bfloat16)
    mixed = lax.all_gather(local_mixed, "mp", axis=2, tiled=True)
    scaled = valid[None, :, None] * cotangent.astype(jnp.float32) / count[None, :, None]
    stitch_part = jnp.einsum("trc,urc->tuc", scaled, hidden, precision=hp)
    through = jnp.einsum("tuc,trc->urc", stitch, scaled, precision=hp)
    dpre = gelu_back(through)[0].astype(jnp.bfloat16)
    bias_part = jnp.sum(dpre.astype(jnp.float32), axis=1)
    weight_part = jnp.einsum("trk,trc->tkc", features, dpre, preferred_element_type=jnp.float32)
    terms = jnp.einsum("trc,tkc->trk", dpre, weights, preferred_element_type=jnp.float32)
    input_sum = lax.psum_scatter(terms, "mp", scatter_dimension=2, tiled=True)
    weight_grad, bias_grad, stitch_grad = lax.psum((weight_part, bias_part, stitch_part), "batch")
    return (mixed, input_sum.astype(jnp.bfloat16), weight_grad, bias_grad, stitch_grad)


def solution(mesh):
    square = mesh.shape["batch"] == GROUP and mesh.shape["mp"] == 2 * LAYERS
    return jax.shard_map(
        packed_body if square else plain_body,
        mesh=mesh,
        in_specs=(
            P(None, "batch", "mp"),
            P(None, None, "mp"),
            P(None, "mp"),
            P(None, None, "mp"),
            P("batch"),
            P("batch"),
            P(None, "batch", "mp"),
        ),
        out_specs=(
            P(None, "batch", None),
            P(None, "batch", "mp"),
            P(None, None, "mp"),
            P(None, "mp"),
            P(None, None, "mp"),
        ),
        check_vma=False,
    )
```

```python
import functools

import jax
import jax.numpy as jnp
from jax import lax
from jax.experimental import pallas as pl
from jax.experimental.pallas import tpu as pltpu
from jax.sharding import PartitionSpec as P

MESH = pl.DeviceIdType.MESH
F32 = jnp.float32
BF16 = jnp.bfloat16
LAYERS = 4
GROUP = 4
TASKS = 2
TANH_SCALE = 0.7978845608
TANH_CUBE = 0.044715

VIA_LAYERS = ((0, 0), (0, 3))
ORDER = (
    ("share", 0, 0), ("own", 0), ("share", 1, 0), ("layer", 0, 1), ("square", 0, 0), ("share", 0, 1), ("layer", 0, 2),
    ("own", 1), ("forward", 0, 0), ("forward", 0, 2), ("share", 0, 2), ("layer", 0, 3), ("corner", 0, 0),
    ("forward", 0, 1), ("forward", 0, 3), ("activate", 0), ("core_terms", 0), ("layer", 1, 1), ("square", 0, 1),
    ("share", 1, 1), ("forward", 1, 0), ("chain", 0, 0), ("share", 0, 3), ("layer", 1, 2), ("chain", 0, 1),
    ("square", 0, 2), ("dpre", 0), ("chain", 0, 2), ("share", 1, 2), ("corner", 0, 1), ("forward", 1, 2),
    ("layer", 1, 3), ("forward", 1, 1), ("share", 1, 3), ("forward", 1, 3), ("activate", 1), ("chain", 0, 3),
    ("core_terms", 1), ("corner", 0, 2), ("square", 1, 1), ("chain", 1, 0), ("square", 1, 0), ("mixed", 1),
    ("square", 0, 3), ("places",), ("gradient", 0, 1), ("square", 1, 2), ("gradient", 0, 0), ("chain", 1, 1),
    ("gradient", 0, 2), ("chain", 1, 2), ("corner", 0, 3), ("dpre", 1), ("corner", 1, 0), ("square", 1, 3),
    ("gradient", 0, 3), ("mixed", 2), ("corner", 1, 1), ("gradient", 1, 0), ("corner", 1, 2), ("gradient", 1, 1),
    ("mixed", 3), ("chain", 1, 3), ("corner", 1, 3),
)


def row_weights(crops, row_mask):
    slots = jnp.arange(row_mask.shape[0], dtype=jnp.int32)
    ends = jnp.cumsum(crops)
    image = jnp.sum((slots[:, None] >= ends[None, :]).astype(jnp.int32), axis=1)
    inside = slots < ends[-1]
    onehot = (image[:, None] == jnp.arange(crops.shape[0], dtype=jnp.int32)[None, :]).astype(
        jnp.int32
    )
    count = jnp.sum(onehot * crops[None, :], axis=1)
    count = jnp.where(inside, count, 1).astype(jnp.float32)
    valid = (row_mask * inside.astype(jnp.int32)).astype(jnp.float32)
    return (count, valid)


def exchange(pool, w, bias, stitch, crops, mask, first, cotangent, xg, dg, mg, ig, st, place, wg,
             wv, pre, dpv, mxv, gx, xc, cot, dgv, gout, scale, acc, sbuf, rup, rdn, tso, tsi, stv,
             wsem, lsem, osem, z_r, z_u, z_d, o_x, o_y, r_x, r_y, r_d, f_s, c_r, c_s,
             dp_s, dp_r, m_r, m_u, m_d, mc_r, mc_s, t_u, t_d, t_s, tc_r, tc_s, st_s, st_r, ig_s, go_s, v_u, v_d):
    rows, depth = xc.shape[1], xc.shape[2]
    cols, slots, images = w.shape[2], mask.shape[1], crops.shape[1]
    b, m = lax.axis_index("batch"), lax.axis_index("mp")
    z, c = m // 2, m % 2
    y, x = b // 2, b % 2
    bx, by, bd = y * 2 + (1 - x), (1 - y) * 2 + x, 3 - b
    to_x, to_y, to_d = (bx, m), (by, m), (bd, m)
    to_c = (b, z * 2 + 1 - c)
    up, down = (b, m + 2), (b, m - 2)
    not_top, not_bottom = z < LAYERS - 1, z > 0
    everyone = [(None, to_x), (None, to_y), (None, to_d), (None, to_c), (not_top, up), (not_bottom, down)]

    barrier = pltpu.get_barrier_semaphore()
    for cond, dev in everyone:
        def greet(dev=dev):
            pl.semaphore_signal(barrier, inc=1, device_id=dev, device_id_type=MESH)
        greet() if cond is None else pl.when(cond)(greet)
    drains = []
    lends = []

    def give_back():
        for drain in lends:
            drain()
        lends.clear()

    def remote(src, dst, send, recv, dev):
        return pltpu.make_async_remote_copy(
            src_ref=src, dst_ref=dst, send_sem=send, recv_sem=recv, device_id=dev, device_id_type=MESH)

    def send(src, dst, ssem, rsem, dev, cond=None):
        def go():
            remote(src, dst, ssem, rsem, dev).start()
        def drain():
            remote(src, dst, ssem, rsem, dev).wait_send()
        if cond is None:
            go()
            drains.append(drain)
        else:
            pl.when(cond)(go)
            drains.append(lambda: pl.when(cond)(drain))

    def arrived(dst, rsem, cond=None):
        def go():
            remote(dst, dst, rsem, rsem, to_c).wait_recv()
        go() if cond is None else pl.when(cond)(go)

    def local(src, dst, sem):
        copy = pltpu.make_async_copy(src, dst, sem)
        copy.start()
        drains.append(copy.wait)
        return copy

    def span(who):
        return pl.ds(pl.multiple_of(who * rows, 16), rows)

    def slot(t, layer, plane, who):
        return xg.at[layer * 2 + plane, t, span(who), :]

    load_w = pltpu.make_async_copy(w, wv, wsem)
    load_pool = [pltpu.make_async_copy(pool.at[t], gx.at[t, pl.ds(0, slots), :], lsem.at[t]) for t in range(TASKS)]

    def grid(shape, axis):
        return lax.broadcasted_iota(jnp.int32, shape, axis).astype(F32)

    def row_weights():
        square = (images, images)
        wide = jnp.broadcast_to(crops[...].astype(F32), square)
        lane, sub = grid(square, 1), grid(square, 0)
        end = jnp.sum(jnp.where(lane <= sub, wide, 0.0), axis=1, keepdims=True)
        crop = jnp.sum(jnp.where(lane == sub, wide, 0.0), axis=1, keepdims=True)
        at = grid((images, slots), 1)
        inside = jnp.where((at < end) & (at >= end - crop), 1.0, 0.0)
        count = jnp.sum(inside * crop, axis=0, keepdims=True)
        valid = mask[...].astype(F32) * jnp.sum(inside, axis=0, keepdims=True)
        return valid, valid / jnp.maximum(count, 1.0)

    def pack():
        valid, weight = row_weights()
        square = (slots, slots)
        upto = jnp.where(grid(square, 0) <= grid(square, 1), 1.0, 0.0).astype(BF16)
        many = jnp.broadcast_to(valid, (16, slots)).astype(BF16)
        index = jnp.dot(many, upto, preferred_element_type=F32)[0:1, :] - 1.0 - first[...].astype(F32)
        pick = jnp.where((grid((rows, slots), 0) == index) & (valid > 0.0), 1.0, 0.0)
        scale[...] = jnp.sum(pick * weight, axis=1, keepdims=True)
        stv[b, 6:7, :] = jnp.broadcast_to(jnp.sum(valid, axis=1, keepdims=True), (1, cols))
        stv[b, 7:8, :] = jnp.zeros((1, cols), F32)
        pick = pick.astype(BF16)
        for t in range(TASKS):
            load_pool[t].wait()
            xc[t] = jnp.dot(pick, gx[t, 0:slots, :], preferred_element_type=F32).astype(BF16)
        for t in range(TASKS):
            cot[t] = jnp.dot(pick, cotangent[t], preferred_element_type=F32).astype(BF16)

    def places():
        valid, _ = row_weights()
        square = (slots, slots)
        wide = jnp.broadcast_to(valid, square)
        lane, sub = grid(square, 1), grid(square, 0)
        index = jnp.sum(jnp.where(lane <= sub, wide, 0.0), axis=1, keepdims=True) - 1.0 - first[...].astype(F32)
        here = jnp.sum(jnp.where(lane == sub, wide, 0.0), axis=1, keepdims=True)
        place[...] = jnp.where((grid((slots, rows), 1) == index) & (here > 0.0), 1.0, 0.0).astype(BF16)

    own = [pltpu.make_async_copy(xc.at[t], slot(t, z, c, b), osem.at[t]) for t in range(TASKS)]

    def own_z(t):
        send(xc.at[t], slot(t, z, c, b), z_u.at[t, z], z_r.at[t, z], up, not_top)
        send(xc.at[t], slot(t, z, c, b), z_d.at[t, z], z_r.at[t, z], down, not_bottom)

    def to_core(t, src, layer, cond=None):
        send(src, slot(t, layer, c, b), c_s.at[0, t, layer], c_r.at[0, t, layer], to_c, cond)

    def to_square(t, src, layer, cond=None):
        send(src, slot(t, layer, c, b), o_x.at[t, layer], r_x.at[t, layer], to_x, cond)
        send(src, slot(t, layer, c, b), o_y.at[t, layer], r_y.at[t, layer], to_y, cond)

    def near(d):
        return [(z, None)] if d == 0 else [(z - d, z >= d), (z + d, z < LAYERS - d)]

    def z_step(t, d):
        (low, is_low), (high, is_high) = near(d)
        here = slot(t, low, c, b)
        arrived(here, z_r.at[t, low], is_low)
        send(here, here, z_u.at[t, low], z_r.at[t, low], up, is_low & not_top)
        to_core(t, here, low, is_low)
        there = slot(t, high, c, b)
        arrived(there, z_r.at[t, high], is_high)
        send(there, there, z_d.at[t, high], z_r.at[t, high], down, is_high & not_bottom)
        to_core(t, there, high, is_high)

    def square_sends(t, d):
        for layer, cond in near(d):
            to_square(t, xc.at[t] if d == 0 else slot(t, layer, c, b), layer, cond)

    def via_layers(t, layer):
        hit = [layer == chosen for task, chosen in VIA_LAYERS if task == t]
        return functools.reduce(lambda p, q: p | q, hit) if hit else None

    def square_step(t, d):
        for layer, cond in near(d):
            from_x, from_y = slot(t, layer, c, bx), slot(t, layer, c, by)
            even, odd = (t + layer) % 2 == 0, (t + layer) % 2 == 1
            if cond is not None:
                even, odd = even & cond, odd & cond
            if d > 0 and via_layers(t, layer) is not None:
                around = jnp.logical_not(via_layers(t, layer))
                even, odd = even & around, odd & around
            arrived(from_x, r_x.at[t, layer], cond)
            send(from_x, from_x, f_s.at[t, layer], r_d.at[t, layer], to_y, even)
            send(from_x, from_x, c_s.at[1, t, layer], c_r.at[1, t, layer], to_c, cond)
            arrived(from_y, r_y.at[t, layer], cond)
            send(from_y, from_y, f_s.at[t, layer], r_d.at[t, layer], to_x, odd)
            send(from_y, from_y, c_s.at[2, t, layer], c_r.at[2, t, layer], to_c, cond)

    def corner_step(t, d):
        for layer, cond in near(d):
            from_d = slot(t, layer, c, bd)
            arrived(from_d, r_d.at[t, layer], cond)
            on = via_layers(t, layer)
            if on is not None:
                send(from_d, from_d, v_u.at[t, layer], r_d.at[t, layer], up, on & (layer <= z) & not_top)
                send(from_d, from_d, v_d.at[t, layer], r_d.at[t, layer], down, on & (layer >= z) & not_bottom)
            send(from_d, from_d, c_s.at[3, t, layer], c_r.at[3, t, layer], to_c, cond)

    def forward(t, d):
        def load(mm, k):
            return pltpu.make_async_copy(xg.at[mm, t, span(b), :], gx.at[k, pl.ds(0, rows), :], lsem.at[k])

        def add(mm, k, source):
            part = pl.ds(pl.multiple_of(mm * depth, 128), depth)
            for h in range(2):
                half = slice(h * (cols // 2), (h + 1) * (cols // 2))
                pre[t, :, half] += jnp.dot(source, wv[t, part, half], preferred_element_type=F32)

        for layer, cond in near(d):
            def go(layer=layer):
                arrived(slot(t, layer, 1 - c, b), c_r.at[0, t, layer])
                load(layer * 2 + 1 - c, 1).start()
                if d == 0:
                    add(layer * 2 + c, 0, xc[t])
                else:
                    load(layer * 2 + c, 0).start()
                    load(layer * 2 + c, 0).wait()
                    add(layer * 2 + c, 0, gx[0, 0:rows, :])
                load(layer * 2 + 1 - c, 1).wait()
                add(layer * 2 + 1 - c, 1, gx[1, 0:rows, :])
            go() if cond is None else pl.when(cond)(go)

    def fold(v):
        return jnp.sum(v.reshape(2, 8, v.shape[1]), axis=0)

    def activate(u):
        def chunk(i, sums):
            s0, s1, bb = sums
            part = pl.ds(pl.multiple_of(i * 16, 16), 16)
            v = pre[u, part, :]
            th = jnp.tanh(TANH_SCALE * (v + TANH_CUBE * (v * v * v)))
            h = 0.5 * v * (1.0 + th)
            slope = 0.5 * (1.0 + th) + 0.5 * v * (1.0 - th * th) * (TANH_SCALE * (1.0 + 3.0 * TANH_CUBE * (v * v)))
            sc = scale[part, :]
            g0 = cot[0, part, :].astype(F32) * sc
            g1 = cot[1, part, :].astype(F32) * sc
            dpre = (slope * (stitch[u:u + 1, :] * g0 + stitch[2 + u:3 + u, :] * g1)).astype(BF16)
            dpv[u, part, :] = dpre
            if u == 0:
                pre[0, part, :] = h
            else:
                h0 = pre[0, part, :]
                for t in range(TASKS):
                    mxv[t, part, :] = (stitch[2 * t:2 * t + 1, :] * h0 + stitch[2 * t + 1:2 * t + 2, :] * h).astype(BF16)
            return s0 + fold(g0 * h), s1 + fold(g1 * h), bb + fold(dpre.astype(F32))

        zero = jnp.zeros((8, cols), F32)
        s0, s1, bb = lax.fori_loop(0, rows // 16, chunk, (zero, zero, zero))
        stv[b, u:u + 1, :] = jnp.sum(s0, axis=0, keepdims=True)
        stv[b, 2 + u:3 + u, :] = jnp.sum(s1, axis=0, keepdims=True)
        stv[b, 4 + u:5 + u, :] = jnp.sum(bb, axis=0, keepdims=True)

    def spread_dpre(t):
        mine = dg.at[t, span(b), :]
        pltpu.make_async_copy(dpv.at[t], mine, dp_s.at[t, 3]).start()
        send(dpv.at[t], mine, dp_s.at[t, 0], dp_r.at[t, 0], to_x)
        send(dpv.at[t], mine, dp_s.at[t, 1], dp_r.at[t, 1], to_y)

    def forward_dpre(t):
        from_x, from_y = dg.at[t, span(bx), :], dg.at[t, span(by), :]
        arrived(from_x, dp_r.at[t, 0])
        arrived(from_y, dp_r.at[t, 1])
        if t == 0:
            send(from_x, from_x, dp_s.at[t, 2], dp_r.at[t, 2], to_y)
        else:
            send(from_y, from_y, dp_s.at[t, 2], dp_r.at[t, 2], to_x)

    def own_mixed():
        local(mxv, mg.at[m], mc_s.at[LAYERS])
        send(mxv, mg.at[m], m_u.at[z], m_r.at[z], up, not_top)
        send(mxv, mg.at[m], m_d.at[z], m_r.at[z], down, not_bottom)
        send(mxv, mg.at[m], mc_s.at[z], mc_r.at[z], to_c)

    def mixed_step(d):
        low, high = z - d, z + d
        here = mg.at[low * 2 + c]
        arrived(here, m_r.at[low], z >= d)
        send(here, here, m_u.at[low], m_r.at[low], up, (z >= d) & not_top)
        send(here, here, mc_s.at[low], mc_r.at[low], to_c, z >= d)
        there = mg.at[high * 2 + c]
        arrived(there, m_r.at[high], z < LAYERS - d)
        send(there, there, m_d.at[high], m_r.at[high], down, (z < LAYERS - d) & not_bottom)
        send(there, there, mc_s.at[high], mc_r.at[high], to_c, z < LAYERS - d)

    tiles = 3
    width = depth // tiles

    def term(t, mm, j):
        part = pl.ds(pl.multiple_of(mm * depth + j * width, 128), width)
        return lax.dot_general(dpv[t], wv[t, part, :], (((1,), (1,)), ((), ())), preferred_element_type=F32)

    def core_terms(t):
        def step(s, carry):
            for j in range(tiles):
                tso[s, :, j * width:(j + 1) * width] = term(t, 2 * s + 1 - c, j).astype(BF16)
            remote(tso.at[s], tsi.at[t, s], tc_s.at[t, s], tc_r.at[t, s], to_c).start()
            return carry

        lax.fori_loop(0, LAYERS, step, 0)
        for s in range(LAYERS):
            lends.append(lambda s=s: remote(
                tso.at[s], tsi.at[t, s], tc_s.at[t, s], tc_r.at[t, s], to_c).wait_send())

    def chain_step(t, k):
        s = [3 * (1 - z // 2), (2 + 3 * z) % 5, 1 + z % 2, z][k]
        has_up = (s >= z) & not_bottom
        has_down = (s <= z) & not_top
        arrived(tsi.at[t, s], tc_r.at[t, s])
        arrived(rup.at[t, s - 1], t_u.at[t, s], has_up)
        arrived(rdn.at[t, s], t_d.at[t, s], has_down)
        for j in range(tiles):
            part = slice(j * width, (j + 1) * width)
            acc[...] = term(t, 2 * s + c, j) + tsi[t, s, :, part].astype(F32)

            @pl.when(has_up)
            def _():
                acc[...] += rup[t, s - 1, :, part].astype(F32)

            @pl.when(has_down)
            def _():
                acc[...] += rdn[t, s, :, part].astype(F32)

            sbuf[s, :, part] = acc[...].astype(BF16)
        before = len(drains)
        if k < LAYERS - 1:
            send(sbuf.at[s], rup.at[t, s - 1], t_s.at[t, s], t_u.at[t, s], up, s > z)
            send(sbuf.at[s], rdn.at[t, s], t_s.at[t, s], t_d.at[t, s], down, s < z)
        else:
            local(sbuf.at[s], ig.at[t], ig_s.at[t])
        lends.extend(drains[before:])
        del drains[before:]

    def all_dpre(t):
        arrived(dg.at[t, span(bd), :], dp_r.at[t, 2])
        pltpu.make_async_copy(dpv.at[t], dg.at[t, span(b), :], dp_s.at[t, 3]).wait()
        load = pltpu.make_async_copy(dg.at[t], dgv, lsem.at[0])
        load.start()
        load.wait()

    def all_pieces(t, layer):
        for k, who in ((1, bx), (2, by), (3, bd)):
            arrived(slot(t, layer, 1 - c, who), c_r.at[k, t, layer])

    def gradient(t, low, many):
        def load(i):
            return pltpu.make_async_copy(xg.at[low + i, t], gx.at[i % 2], lsem.at[i % 2])

        def store(i):
            return pltpu.make_async_copy(gout.at[i % 2], wg.at[t, low + i], go_s.at[i % 2])

        load(0).start()

        def step(i, carry):
            k = i % 2
            pl.when(i + 1 < many)(lambda: load(i + 1).start())
            load(i).wait()
            pl.when(i >= 2)(lambda: store(i - 2).wait())
            for j in range(tiles):
                part = slice(j * width, (j + 1) * width)
                gout[k, part, :] = lax.dot_general(
                    gx[k, :, part], dgv[...], (((0,), (0,)), ((), ())), preferred_element_type=F32).astype(BF16)
            store(i).start()
            return carry

        lax.fori_loop(0, many, step, 0)
        for i in range(max(0, many - 2), many):
            store(i).wait()

    def places_step():
        places()
        for copy in own:
            copy.start()

    def own_step(t):
        own_z(t)
        to_core(t, xc.at[t], z)

    def activate_step(t):
        activate(t)
        spread_dpre(t)
        if t == 1:
            own_mixed()
            send(stv.at[b], stv.at[b], st_s.at[0], st_r.at[0], to_x)
            send(stv.at[b], stv.at[b], st_s.at[1], st_r.at[1], to_y)
            send(stv.at[b], stv.at[b], st_s.at[2], st_r.at[2], to_d)

    def core_step(t):
        give_back()
        core_terms(t)

    ready = []

    def gradient_step(t, j):
        layer = [z, z + 1 - 2 * (z % 2), 2 - z // 2, 3 * (1 - z // 2)][j]
        if t not in ready:
            ready.append(t)
            for copy in own:
                copy.wait()
            own.clear()
            all_dpre(t)
        all_pieces(t, layer)
        gradient(t, 2 * layer, 2)

    for copy in load_pool:
        copy.start()
    load_w.start()
    pack()
    for t in range(TASKS):
        pre[t] = jnp.broadcast_to(bias[t:t + 1, :], (rows, cols))
    ends = LAYERS - 1
    pl.semaphore_wait(barrier, 4 + (z + ends - 1) // ends + (2 * ends - 1 - z) // ends)
    steps = {
        "places": places_step, "own": own_step, "layer": z_step, "share": square_sends, "forward": forward,
        "activate": activate_step, "core_terms": core_step, "chain": chain_step, "square": square_step,
        "corner": corner_step, "dpre": forward_dpre, "mixed": mixed_step, "gradient": gradient_step,
    }
    loaded = False
    for name, *at in ORDER:
        if name == "forward" and not loaded:
            load_w.wait()
            loaded = True
        steps[name](*at)
    done = [at[1] for name, *at in ORDER if name == "gradient" and at[0] == 1]
    for j in range(LAYERS):
        if j not in done:
            all_pieces(1, [z, z + 1 - 2 * (z % 2), 2 - z // 2, 3 * (1 - z // 2)][j])
    for layer in range(LAYERS):
        arrived(mg.at[layer * 2 + 1 - c], mc_r.at[layer])
    arrived(stv.at[bx], st_r.at[0])
    arrived(stv.at[by], st_r.at[1])
    arrived(stv.at[bd], st_r.at[2])
    give_back()
    for drain in drains:
        drain()
    st[...] = stv[...]


def run_exchange(pool_in, weights, bias, stitch, crops, mask, first, cotangent, rows):
    tasks, slots, depth = pool_in.shape
    cols = weights.shape[2]
    parts = weights.shape[1] // depth
    sem = pltpu.SemaphoreType.DMA
    any_spec = pl.BlockSpec(memory_space=pl.ANY)
    vmem_spec = pl.BlockSpec(memory_space=pltpu.VMEM)
    two, four = TASKS, LAYERS
    piece = (rows, depth)
    return pl.pallas_call(
        exchange,
        out_shape=(
            jax.ShapeDtypeStruct((parts, tasks, GROUP * rows, depth), BF16),
            jax.ShapeDtypeStruct((tasks, GROUP * rows, cols), BF16),
            jax.ShapeDtypeStruct((parts, tasks, rows, cols), BF16),
            jax.ShapeDtypeStruct((tasks, rows, depth), BF16),
            jax.ShapeDtypeStruct((GROUP, 8, cols), F32),
            jax.ShapeDtypeStruct((slots, rows), BF16),
            jax.ShapeDtypeStruct((tasks, parts, depth, cols), BF16),
        ),
        in_specs=[any_spec, any_spec] + [vmem_spec] * 6,
        out_specs=(any_spec, any_spec, any_spec, any_spec, vmem_spec, vmem_spec, any_spec),
        scratch_shapes=[
            pltpu.VMEM(weights.shape, BF16),
            pltpu.VMEM((tasks, rows, cols), F32),
            pltpu.VMEM((tasks, rows, cols), BF16),
            pltpu.VMEM((tasks, rows, cols), BF16),
            pltpu.VMEM((2, GROUP * rows, depth), BF16),
            pltpu.VMEM((tasks, *piece), BF16),
            pltpu.VMEM((tasks, rows, cols), BF16),
            pltpu.VMEM((GROUP * rows, cols), BF16),
            pltpu.VMEM((2, depth, cols), BF16),
            pltpu.VMEM((rows, 1), F32),
            pltpu.VMEM((rows, depth // 3), F32),
            pltpu.VMEM((LAYERS, *piece), BF16),
            pltpu.VMEM((tasks, LAYERS - 1, *piece), BF16),
            pltpu.VMEM((tasks, LAYERS - 1, *piece), BF16),
            pltpu.VMEM((LAYERS, *piece), BF16),
            pltpu.VMEM((tasks, LAYERS, *piece), BF16),
            pltpu.VMEM((GROUP, 8, cols), F32),
            sem, sem((2,)), sem((two,)),
            sem((two, four)), sem((two, four)), sem((two, four)),
            sem((two, four)), sem((two, four)), sem((two, four)), sem((two, four)), sem((two, four)),
            sem((two, four)), sem((4, two, four)), sem((4, two, four)),
            sem((two, 4)), sem((two, 3)),
            sem((four,)), sem((four,)), sem((four,)), sem((four,)), sem((four + 1,)),
            sem((two, four)), sem((two, four)), sem((two, four)), sem((two, four)), sem((two, four)),
            sem((3,)), sem((3,)), sem((two,)), sem((2,)), sem((two, four)), sem((two, four)),
        ],
        compiler_params=pltpu.CompilerParams(
            collective_id=0, has_side_effects=True, vmem_limit_bytes=60 * 1024 * 1024),
        cost_estimate=pl.CostEstimate(
            flops=8 * tasks * rows * parts * depth * cols, bytes_accessed=150_000_000, transcendentals=0),
    )(pool_in, weights, bias, stitch, crops, mask, first, cotangent)


def block_of(p, t, half_ref):
    half = pl.num_programs(0) // 2
    late = (p % 2) * t
    own = p // 2 + half * ((half_ref[0] + late) % 2)
    return t * own + (1 - t) * p


def finish(count, half_ref, *refs):
    ins, (mixed, input_grad, weight_grad) = refs[:6 * count], refs[6 * count:]
    p, t = pl.program_id(0), pl.program_id(1)
    late = (t == 1) & (p % 2 == 1)
    for k in range(count):
        xg, dg, mg, ig, place, wg = ins[6 * k:6 * k + 6]

        def put(ref, value, where=(0,)):
            if k == 0:
                ref[where] = value.astype(ref.dtype)
            else:
                ref[where] += value.astype(ref.dtype)

        @pl.when(late)
        def _():
            put(weight_grad, lax.dot_general(
                xg[0, 0], dg[0], (((0,), (0,)), ((), ())), preferred_element_type=F32))

        @pl.when(jnp.logical_not(late))
        def _():
            put(weight_grad, wg[0, 0].astype(F32))

        put(mixed, jnp.dot(place[...], mg[0, 0], preferred_element_type=F32))

        @pl.when(p == 0)
        def _():
            put(input_grad, jnp.dot(place[...], ig[t], preferred_element_type=F32), (t,))


def run_finish(passes, half):
    xg, dg, mg, ig, _, place, wg = passes[0]
    slots, rows = place.shape
    parts, tasks, all_rows, depth = xg.shape
    cols = dg.shape[2]

    def late_block(p, t, h):
        return (p // 2 + parts // 2 * ((h[0] + 1) % 2), 1, 0, 0)

    def early_block(p, t, h):
        late = (p % 2) * t
        return (t * (1 - late), late * p + (1 - late) * block_of(p, t, h), 0, 0)

    in_specs = [
        pl.BlockSpec((1, 1, all_rows, depth), late_block),
        pl.BlockSpec((1, all_rows, cols), lambda p, t, h: (1, 0, 0)),
        pl.BlockSpec((1, 1, rows, cols), lambda p, t, h: (block_of(p, t, h), t, 0, 0)),
        pl.BlockSpec((tasks, rows, depth), lambda p, t, h: (0, 0, 0)),
        pl.BlockSpec((slots, rows), lambda p, t, h: (0, 0)),
        pl.BlockSpec((1, 1, depth, cols), early_block),
    ]
    flops = 2 * tasks * parts * cols * (all_rows * depth // 4 + slots * rows)
    return pl.pallas_call(
        functools.partial(finish, len(passes)),
        grid_spec=pltpu.PrefetchScalarGridSpec(
            num_scalar_prefetch=1,
            grid=(parts, tasks),
            in_specs=in_specs * len(passes),
            out_specs=(
                pl.BlockSpec((1, slots, cols), lambda p, t, h: (t, 0, block_of(p, t, h))),
                pl.BlockSpec((tasks, slots, depth), lambda p, t, h: (0, 0, 0)),
                pl.BlockSpec((1, depth, cols), lambda p, t, h: (t, block_of(p, t, h), 0)),
            ),
        ),
        out_shape=(
            jax.ShapeDtypeStruct((tasks, slots, parts * cols), BF16),
            jax.ShapeDtypeStruct((tasks, slots, depth), BF16),
            jax.ShapeDtypeStruct((tasks, parts * depth, cols), F32),
        ),
        compiler_params=pltpu.CompilerParams(vmem_limit_bytes=60 * 1024 * 1024),
        cost_estimate=pl.CostEstimate(flops=flops, bytes_accessed=75_000_000, transcendentals=0),
    )(half, *[v for out in passes for v in (*out[:4], out[5], out[6])])


def packed_body(pool_in, weights, bias, stitch, crops, row_mask, cotangent):
    slots = row_mask.shape[0]
    cols = weights.shape[2]
    rows = (slots * 17 // 32 + 15) // 16 * 16
    units = stitch.reshape(TASKS * TASKS, cols)

    def part(first):
        return run_exchange(pool_in, weights, bias, units, crops.reshape(1, -1), row_mask.reshape(1, -1),
                            jnp.full((1, 1), first, jnp.int32), cotangent, rows)

    def results(passes):
        half = (lax.axis_index("mp") // LAYERS).astype(jnp.int32).reshape(1)
        mixed, input_grad, weight_grad = run_finish(passes, half)
        small = sum(jnp.sum(out[4], axis=0) for out in passes)
        return (mixed, input_grad, weight_grad, small[4:6], small[0:4].reshape(TASKS, TASKS, cols))

    front = part(0)
    most = jnp.max(front[4][:, 6, 0])
    return lax.cond(most > rows, lambda: results([front, part(rows)]), lambda: results([front]))


def plain_body(pool_in, weights, bias, stitch, crops, row_mask, cotangent):
    hp = lax.Precision.HIGHEST
    count, valid = row_weights(crops, row_mask)
    features = lax.all_gather(pool_in, "mp", axis=2, tiled=True)
    linear = jnp.einsum("trk,tkc->trc", features, weights, preferred_element_type=jnp.float32)
    pre = linear + bias[:, None, :]
    hidden, gelu_back = jax.vjp(jax.nn.gelu, pre)
    stitched = stitch[:, 0, None, :] * hidden[0][None] + stitch[:, 1, None, :] * hidden[1][None]
    local_mixed = (valid[None, :, None] * stitched).astype(jnp.bfloat16)
    mixed = lax.all_gather(local_mixed, "mp", axis=2, tiled=True)
    scaled = valid[None, :, None] * cotangent.astype(jnp.float32) / count[None, :, None]
    stitch_part = jnp.einsum("trc,urc->tuc", scaled, hidden, precision=hp)
    through = jnp.einsum("tuc,trc->urc", stitch, scaled, precision=hp)
    dpre = gelu_back(through)[0].astype(jnp.bfloat16)
    bias_part = jnp.sum(dpre.astype(jnp.float32), axis=1)
    weight_part = jnp.einsum("trk,trc->tkc", features, dpre, preferred_element_type=jnp.float32)
    terms = jnp.einsum("trc,tkc->trk", dpre, weights, preferred_element_type=jnp.float32)
    input_sum = lax.psum_scatter(terms, "mp", scatter_dimension=2, tiled=True)
    weight_grad, bias_grad, stitch_grad = lax.psum((weight_part, bias_part, stitch_part), "batch")
    return (mixed, input_sum.astype(jnp.bfloat16), weight_grad, bias_grad, stitch_grad)


def solution(mesh):
    square = mesh.shape["batch"] == GROUP and mesh.shape["mp"] == 2 * LAYERS
    return jax.shard_map(
        packed_body if square else plain_body,
        mesh=mesh,
        in_specs=(
            P(None, "batch", "mp"),
            P(None, None, "mp"),
            P(None, "mp"),
            P(None, None, "mp"),
            P("batch"),
            P("batch"),
            P(None, "batch", "mp"),
        ),
        out_specs=(
            P(None, "batch", None),
            P(None, "batch", "mp"),
            P(None, None, "mp"),
            P(None, "mp"),
            P(None, None, "mp"),
        ),
        check_vma=False,
    )
```

```python
import functools

import jax
import jax.numpy as jnp
from jax import lax
from jax.experimental import pallas as pl
from jax.experimental.pallas import tpu as pltpu
from jax.sharding import PartitionSpec as P

MESH = pl.DeviceIdType.MESH
F32 = jnp.float32
BF16 = jnp.bfloat16
LAYERS = 4
GROUP = 4
TASKS = 2
TANH_SCALE = 0.7978845608
TANH_CUBE = 0.044715

CORNER_LATER = ((1, 2), (1, 3))
HALVED = ()
VIA_LAYERS = ((0, 0), (0, 3))
ORDER = (
    ("share", 0, 0), ("own", 0), ("share", 1, 0), ("layer", 0, 1), ("square", 0, 0), ("share", 0, 1), ("layer", 0, 2),
    ("forward", 0, 0), ("share", 0, 2), ("own", 1), ("forward", 0, 1), ("layer", 0, 3), ("forward", 0, 2),
    ("corner", 0, 0), ("forward", 0, 3), ("activate", 0), ("core_terms", 0), ("layer", 1, 1), ("square", 0, 1),
    ("square", 1, 0), ("chain", 0, 0), ("layer", 1, 2), ("square", 0, 2), ("forward", 1, 2), ("forward", 1, 1),
    ("chain", 0, 1), ("dpre", 0), ("corner", 0, 1), ("share", 1, 1), ("chain", 0, 2), ("forward", 1, 0),
    ("layer", 1, 3), ("share", 0, 3), ("forward", 1, 3), ("activate", 1), ("gradient", 0, 1), ("corner", 0, 2),
    ("share", 1, 2), ("chain", 0, 3), ("core_terms", 1), ("gradient", 0, 0), ("chain", 1, 0), ("mixed", 1),
    ("gradient", 0, 2), ("dpre", 1), ("corner", 1, 0), ("square", 0, 3), ("corner", 0, 3), ("places",),
    ("share", 1, 3), ("square", 1, 1), ("gradient", 0, 3), ("chain", 1, 1), ("square", 1, 2), ("gradient", 1, 0),
    ("square", 1, 3), ("chain", 1, 2), ("mixed", 2), ("gradient", 1, 2), ("gradient", 1, 3), ("corner", 1, 1),
    ("corner", 1, 2), ("chain", 1, 3), ("gradient", 1, 1), ("mixed", 3), ("corner", 1, 3),
)


def row_weights(crops, row_mask):
    slots = jnp.arange(row_mask.shape[0], dtype=jnp.int32)
    ends = jnp.cumsum(crops)
    image = jnp.sum((slots[:, None] >= ends[None, :]).astype(jnp.int32), axis=1)
    inside = slots < ends[-1]
    onehot = (image[:, None] == jnp.arange(crops.shape[0], dtype=jnp.int32)[None, :]).astype(
        jnp.int32
    )
    count = jnp.sum(onehot * crops[None, :], axis=1)
    count = jnp.where(inside, count, 1).astype(jnp.float32)
    valid = (row_mask * inside.astype(jnp.int32)).astype(jnp.float32)
    return (count, valid)


def exchange(pool, w, bias, stitch, crops, mask, first, cotangent, xg, dg, mg, ig, st, place, wg, at,
             wv, pre, dpv, mxv, gx, xc, cot, dgv, dgt, gout, scale, acc, sbuf, rup, rdn, tso, tsi, stv,
             wsem, lsem, osem, z_r, z_u, z_d, o_x, o_y, r_x, r_y, r_d, f_s, c_r, c_s,
             dp_s, dp_r, m_r, m_u, m_d, mc_r, mc_s, t_u, t_d, t_s, tc_r, tc_s, st_s, st_r, ig_s, go_s, v_u, v_d, f_h, r_h):
    rows, depth = xc.shape[1], xc.shape[2]
    cols, slots, images = w.shape[2], mask.shape[1], crops.shape[1]
    b, m = lax.axis_index("batch"), lax.axis_index("mp")
    z, c = m // 2, m % 2
    y, x = b // 2, b % 2
    bx, by, bd = y * 2 + (1 - x), (1 - y) * 2 + x, 3 - b
    to_x, to_y, to_d = (bx, m), (by, m), (bd, m)
    to_c = (b, z * 2 + 1 - c)
    up, down = (b, m + 2), (b, m - 2)
    not_top, not_bottom = z < LAYERS - 1, z > 0
    everyone = [(None, to_x), (None, to_y), (None, to_d), (None, to_c), (not_top, up), (not_bottom, down)]

    barrier = pltpu.get_barrier_semaphore()
    for cond, dev in everyone:
        def greet(dev=dev):
            pl.semaphore_signal(barrier, inc=1, device_id=dev, device_id_type=MESH)
        greet() if cond is None else pl.when(cond)(greet)
    drains = []
    lent = {}

    def give_back(name):
        for drain in lent.pop(name, ()):
            drain()

    def remote(src, dst, send, recv, dev):
        return pltpu.make_async_remote_copy(
            src_ref=src, dst_ref=dst, send_sem=send, recv_sem=recv, device_id=dev, device_id_type=MESH)

    def send(src, dst, ssem, rsem, dev, cond=None):
        def go():
            remote(src, dst, ssem, rsem, dev).start()
        def drain():
            remote(src, dst, ssem, rsem, dev).wait_send()
        if cond is None:
            go()
            drains.append(drain)
        else:
            pl.when(cond)(go)
            drains.append(lambda: pl.when(cond)(drain))

    def arrived(dst, rsem, cond=None):
        def go():
            remote(dst, dst, rsem, rsem, to_c).wait_recv()
        go() if cond is None else pl.when(cond)(go)

    def local(src, dst, sem):
        copy = pltpu.make_async_copy(src, dst, sem)
        copy.start()
        drains.append(copy.wait)
        return copy

    def span(who):
        return pl.ds(pl.multiple_of(who * rows, 16), rows)

    top = (rows // 2 + 15) // 16 * 16
    outer = (z == 0) | (z == LAYERS - 1)
    inner = jnp.logical_not(outer)

    def slot(t, layer, plane, who, half=None):
        part = span(who)
        if half is not None:
            part = pl.ds(pl.multiple_of(who * rows + half * top, 16), rows - top if half else top)
        return xg.at[layer * 2 + plane, t, part, :]

    load_w = pltpu.make_async_copy(w, wv, wsem)
    load_pool = [pltpu.make_async_copy(pool.at[t], gx.at[t, pl.ds(0, slots), :], lsem.at[t]) for t in range(TASKS)]

    def grid(shape, axis):
        return lax.broadcasted_iota(jnp.int32, shape, axis).astype(F32)

    def row_weights():
        square = (images, images)
        wide = jnp.broadcast_to(crops[...].astype(F32), square)
        lane, sub = grid(square, 1), grid(square, 0)
        end = jnp.sum(jnp.where(lane <= sub, wide, 0.0), axis=1, keepdims=True)
        crop = jnp.sum(jnp.where(lane == sub, wide, 0.0), axis=1, keepdims=True)
        at = grid((images, slots), 1)
        inside = jnp.where((at < end) & (at >= end - crop), 1.0, 0.0)
        count = jnp.sum(inside * crop, axis=0, keepdims=True)
        valid = mask[...].astype(F32) * jnp.sum(inside, axis=0, keepdims=True)
        return valid, valid / jnp.maximum(count, 1.0)

    def pack():
        valid, weight = row_weights()
        square = (slots, slots)
        upto = jnp.where(grid(square, 0) <= grid(square, 1), 1.0, 0.0).astype(BF16)
        many = jnp.broadcast_to(valid, (16, slots)).astype(BF16)
        index = jnp.dot(many, upto, preferred_element_type=F32)[0:1, :] - 1.0 - first[...].astype(F32)
        pick = jnp.where((grid((rows, slots), 0) == index) & (valid > 0.0), 1.0, 0.0)
        scale[...] = jnp.sum(pick * weight, axis=1, keepdims=True)
        stv[b, 6:7, :] = jnp.broadcast_to(jnp.sum(valid, axis=1, keepdims=True), (1, cols))
        stv[b, 7:8, :] = jnp.zeros((1, cols), F32)
        pick = pick.astype(BF16)
        for t in range(TASKS):
            load_pool[t].wait()
            xc[t] = jnp.dot(pick, gx[t, 0:slots, :], preferred_element_type=F32).astype(BF16)
        for t in range(TASKS):
            cot[t] = jnp.dot(pick, cotangent[t], preferred_element_type=F32).astype(BF16)

    def places():
        valid, _ = row_weights()
        square = (slots, slots)
        wide = jnp.broadcast_to(valid, square)
        lane, sub = grid(square, 1), grid(square, 0)
        index = jnp.sum(jnp.where(lane <= sub, wide, 0.0), axis=1, keepdims=True) - 1.0 - first[...].astype(F32)
        here = jnp.sum(jnp.where(lane == sub, wide, 0.0), axis=1, keepdims=True)
        place[...] = jnp.where((grid((slots, rows), 1) == index) & (here > 0.0), 1.0, 0.0).astype(BF16)

    own = [pltpu.make_async_copy(xc.at[t], slot(t, z, c, b), osem.at[t]) for t in range(TASKS)]

    def own_z(t):
        send(xc.at[t], slot(t, z, c, b), z_u.at[t, z], z_r.at[t, z], up, not_top)
        send(xc.at[t], slot(t, z, c, b), z_d.at[t, z], z_r.at[t, z], down, not_bottom)

    def to_core(t, src, layer, cond=None):
        send(src, slot(t, layer, c, b), c_s.at[0, t, layer], c_r.at[0, t, layer], to_c, cond)

    def to_square(t, src, layer, cond=None):
        send(src, slot(t, layer, c, b), o_x.at[t, layer], r_x.at[t, layer], to_x, cond)
        send(src, slot(t, layer, c, b), o_y.at[t, layer], r_y.at[t, layer], to_y, cond)

    def near(d):
        return [(z, None)] if d == 0 else [(z - d, z >= d), (z + d, z < LAYERS - d)]

    def z_step(t, d):
        (low, is_low), (high, is_high) = near(d)
        here = slot(t, low, c, b)
        arrived(here, z_r.at[t, low], is_low)
        send(here, here, z_u.at[t, low], z_r.at[t, low], up, is_low & not_top)
        to_core(t, here, low, is_low)
        there = slot(t, high, c, b)
        arrived(there, z_r.at[t, high], is_high)
        send(there, there, z_d.at[t, high], z_r.at[t, high], down, is_high & not_bottom)
        to_core(t, there, high, is_high)

    def square_sends(t, d):
        for layer, cond in near(d):
            to_square(t, xc.at[t] if d == 0 else slot(t, layer, c, b), layer, cond)

    def via_layers(t, layer):
        hit = [layer == chosen for task, chosen in VIA_LAYERS if task == t]
        return functools.reduce(lambda p, q: p | q, hit) if hit else None

    def square_step(t, d):
        for layer, cond in near(d):
            from_x, from_y = slot(t, layer, c, bx), slot(t, layer, c, by)
            even, odd = (t + layer) % 2 == 0, (t + layer) % 2 == 1
            if cond is not None:
                even, odd = even & cond, odd & cond
            if d > 0 and via_layers(t, layer) is not None:
                around = jnp.logical_not(via_layers(t, layer))
                even, odd = even & around, odd & around
            halved = (t, d) in HALVED
            if halved:
                even, odd = even & inner, odd & inner
            arrived(from_x, r_x.at[t, layer], cond)
            send(from_x, from_x, f_s.at[t, layer], r_d.at[t, layer], to_y, even)
            if halved:
                first = slot(t, layer, c, bx, 0)
                send(first, first, f_s.at[t, layer], r_d.at[t, layer], to_y, cond & outer)
            send(from_x, from_x, c_s.at[1, t, layer], c_r.at[1, t, layer], to_c, cond)
            arrived(from_y, r_y.at[t, layer], cond)
            send(from_y, from_y, f_s.at[t, layer], r_d.at[t, layer], to_x, odd)
            if halved:
                second = slot(t, layer, c, by, 1)
                send(second, second, f_h.at[t, layer], r_h.at[t, layer], to_x, cond & outer)
            send(from_y, from_y, c_s.at[2, t, layer], c_r.at[2, t, layer], to_c, cond)

    def corner_step(t, d):
        for layer, cond in near(d):
            from_d = slot(t, layer, c, bd)
            if (t, d) in HALVED:
                arrived(from_d, r_d.at[t, layer], cond & inner)
                arrived(slot(t, layer, c, bd, 0), r_d.at[t, layer], cond & outer)
                arrived(slot(t, layer, c, bd, 1), r_h.at[t, layer], cond & outer)
            else:
                arrived(from_d, r_d.at[t, layer], cond)
            on = via_layers(t, layer)
            if on is not None:
                send(from_d, from_d, v_u.at[t, layer], r_d.at[t, layer], up, on & (layer <= z) & not_top)
                send(from_d, from_d, v_d.at[t, layer], r_d.at[t, layer], down, on & (layer >= z) & not_bottom)
            send(from_d, from_d, c_s.at[3, t, layer], c_r.at[3, t, layer], to_c, cond)

    around = (b, bx, by, bd)

    def strip(i):
        return pl.ds(i * rows, rows)

    def forward(t, d):
        def add(mm, source):
            part = pl.ds(pl.multiple_of(mm * depth, 128), depth)

            def half(h, carry):
                out = pl.ds(pl.multiple_of(h * (cols // 2), 128), cols // 2)
                pre[t, :, out] += jnp.dot(source[...], wv[t, part, out], preferred_element_type=F32)
                return carry

            lax.fori_loop(0, 2, half, 0)

        def fetch(i, layer, plane):
            return pltpu.make_async_copy(
                xg.at[layer * 2 + plane, t, span(b), :], gx.at[plane, strip(i), :], lsem.at[i * 2 + plane])

        sides = near(d)
        if d == 0:
            own[t].wait()
        for i, (layer, cond) in enumerate(sides):
            def begin(i=i, layer=layer):
                arrived(slot(t, layer, 1 - c, b), c_r.at[0, t, layer])
                for plane in range(2):
                    fetch(i, layer, plane).start()
            begin() if cond is None else pl.when(cond)(begin)

        def block(n, carry):
            i, plane = n // 2, n % 2
            layer = z + (2 * i - 1) * d

            @pl.when((layer >= 0) & (layer < LAYERS))
            def _():
                pltpu.make_async_copy(
                    xg.at[layer * 2 + plane, t, span(b), :], gx.at[plane, pl.ds(pl.multiple_of(i * rows, 16), rows), :],
                    lsem.at[n]).wait()
                add(layer * 2 + plane, gx.at[plane, pl.ds(pl.multiple_of(i * rows, 16), rows), :])

            return carry

        lax.fori_loop(0, 2 * len(sides), block, 0)

    def fold(v):
        return jnp.sum(v.reshape(2, 8, v.shape[1]), axis=0)

    def activate(u):
        def chunk(i, sums):
            s0, s1, bb = sums
            part = pl.ds(pl.multiple_of(i * 16, 16), 16)
            v = pre[u, part, :]
            th = jnp.tanh(TANH_SCALE * (v + TANH_CUBE * (v * v * v)))
            h = 0.5 * v * (1.0 + th)
            slope = 0.5 * (1.0 + th) + 0.5 * v * (1.0 - th * th) * (TANH_SCALE * (1.0 + 3.0 * TANH_CUBE * (v * v)))
            sc = scale[part, :]
            g0 = cot[0, part, :].astype(F32) * sc
            g1 = cot[1, part, :].astype(F32) * sc
            dpre = (slope * (stitch[0, u:u + 1, :] * g0 + stitch[1, u:u + 1, :] * g1)).astype(BF16)
            dpv[u, part, :] = dpre
            if u == 0:
                pre[0, part, :] = h
            else:
                h0 = pre[0, part, :]
                for t in range(TASKS):
                    mxv[t, part, :] = (stitch[t, 0:1, :] * h0 + stitch[t, 1:2, :] * h).astype(BF16)
            return s0 + fold(g0 * h), s1 + fold(g1 * h), bb + fold(dpre.astype(F32))

        zero = jnp.zeros((8, cols), F32)
        s0, s1, bb = lax.fori_loop(0, rows // 16, chunk, (zero, zero, zero))
        stv[b, u:u + 1, :] = jnp.sum(s0, axis=0, keepdims=True)
        stv[b, 2 + u:3 + u, :] = jnp.sum(s1, axis=0, keepdims=True)
        stv[b, 4 + u:5 + u, :] = jnp.sum(bb, axis=0, keepdims=True)

    def spread_dpre(t):
        mine = dg.at[t, span(b), :]
        pltpu.make_async_copy(dpv.at[t], mine, dp_s.at[t, 3]).start()
        send(dpv.at[t], mine, dp_s.at[t, 0], dp_r.at[t, 0], to_x)
        send(dpv.at[t], mine, dp_s.at[t, 1], dp_r.at[t, 1], to_y)

    def forward_dpre(t):
        from_x, from_y = dg.at[t, span(bx), :], dg.at[t, span(by), :]
        arrived(from_x, dp_r.at[t, 0])
        arrived(from_y, dp_r.at[t, 1])
        if t == 0:
            send(from_x, from_x, dp_s.at[t, 2], dp_r.at[t, 2], to_y)
        else:
            send(from_y, from_y, dp_s.at[t, 2], dp_r.at[t, 2], to_x)

    def own_mixed():
        local(mxv, mg.at[m], mc_s.at[LAYERS])
        send(mxv, mg.at[m], m_u.at[z], m_r.at[z], up, not_top)
        send(mxv, mg.at[m], m_d.at[z], m_r.at[z], down, not_bottom)
        send(mxv, mg.at[m], mc_s.at[z], mc_r.at[z], to_c)

    def mixed_step(d):
        low, high = z - d, z + d
        here = mg.at[low * 2 + c]
        arrived(here, m_r.at[low], z >= d)
        send(here, here, m_u.at[low], m_r.at[low], up, (z >= d) & not_top)
        send(here, here, mc_s.at[low], mc_r.at[low], to_c, z >= d)
        there = mg.at[high * 2 + c]
        arrived(there, m_r.at[high], z < LAYERS - d)
        send(there, there, m_d.at[high], m_r.at[high], down, (z < LAYERS - d) & not_bottom)
        send(there, there, mc_s.at[high], mc_r.at[high], to_c, z < LAYERS - d)

    tiles = 3
    width = depth // tiles

    def lanes(j):
        return pl.ds(pl.multiple_of(j * width, 128), width)

    def term(t, mm, j):
        part = pl.ds(pl.multiple_of(mm * depth + j * width, 128), width)
        return lax.dot_general(dpv[t], wv[t, part, :], (((1,), (1,)), ((), ())), preferred_element_type=F32)

    def core_terms(t):
        def step(s, carry):
            part = pl.ds(pl.multiple_of((2 * s + 1 - c) * depth, 128), depth)
            tso[s] = lax.dot_general(
                dpv[t], wv[t, part, :], (((1,), (1,)), ((), ())), preferred_element_type=F32).astype(BF16)
            remote(tso.at[s], tsi.at[t, s], tc_s.at[t, s], tc_r.at[t, s], to_c).start()
            return carry

        lax.fori_loop(0, LAYERS, step, 0)
        lent["core"] = [lambda s=s: remote(
            tso.at[s], tsi.at[t, s], tc_s.at[t, s], tc_r.at[t, s], to_c).wait_send() for s in range(LAYERS)]

    def chain_step(t, k):
        s = [3 * (1 - z // 2), (2 + 3 * z) % 5, 1 + z % 2, z][k]
        has_up = (s >= z) & not_bottom
        has_down = (s <= z) & not_top
        give_back(k)
        arrived(tsi.at[t, s], tc_r.at[t, s])
        arrived(rup.at[t, s - 1], t_u.at[t, s], has_up)
        arrived(rdn.at[t, s], t_d.at[t, s], has_down)

        def step(j, carry):
            acc[...] = term(t, 2 * s + c, j) + tsi[t, s, :, lanes(j)].astype(F32)

            @pl.when(has_up)
            def _():
                acc[...] += rup[t, s - 1, :, lanes(j)].astype(F32)

            @pl.when(has_down)
            def _():
                acc[...] += rdn[t, s, :, lanes(j)].astype(F32)

            sbuf[s, :, lanes(j)] = acc[...].astype(BF16)
            return carry

        lax.fori_loop(0, tiles, step, 0)
        before = len(drains)
        if k < LAYERS - 1:
            send(sbuf.at[s], rup.at[t, s - 1], t_s.at[t, s], t_u.at[t, s], up, s > z)
            send(sbuf.at[s], rdn.at[t, s], t_s.at[t, s], t_d.at[t, s], down, s < z)
        else:
            local(sbuf.at[s], ig.at[t], ig_s.at[t])
        lent[k] = drains[before:]
        del drains[before:]

    def all_dpre(t):
        arrived(dg.at[t, span(bd), :], dp_r.at[t, 2])
        pltpu.make_async_copy(dpv.at[t], dg.at[t, span(b), :], dp_s.at[t, 3]).wait()
        loads = [pltpu.make_async_copy(dg.at[t, span(who), :], dgv.at[strip(i), :], lsem.at[i])
                 for i, who in enumerate(around)]
        for copy in loads:
            copy.start()
        for copy in loads:
            copy.wait()
        dgt[...] = dgv[...].T

    def all_pieces(t, layer, corner=True):
        for k, who in ((1, bx), (2, by), (3, bd)):
            if k < 3 or corner:
                arrived(slot(t, layer, 1 - c, who), c_r.at[k, t, layer])

    def corner_pieces(t, layer):
        arrived(slot(t, layer, 1 - c, bd), c_r.at[3, t, layer])

    def gradient(t, layer, corner):
        many = GROUP if corner else GROUP - 1

        def load(k):
            mm = 2 * layer + k
            return [pltpu.make_async_copy(xg.at[mm, t, span(who), :], gx.at[k, strip(i), :], lsem.at[k * GROUP + i])
                    for i, who in enumerate(around[:many])]

        def store(k):
            return pltpu.make_async_copy(gout.at[k], wg.at[t, 2 * layer + k], go_s.at[k])

        for k in range(2):
            for copy in load(k):
                copy.start()
        give_back("gradient")
        wide = 2 * 128
        whole = depth // wide * wide

        def multiply(k, part):
            gout[k, :, part] = jnp.dot(
                dgt[:, 0:many * rows], gx[k, 0:many * rows, part], preferred_element_type=F32).astype(BF16)

        def tile(k, carry):
            for i in range(many):
                pltpu.make_async_copy(
                    xg.at[2 * layer + k, t, span(around[i]), :], gx.at[k, strip(i), :], lsem.at[k * GROUP + i]).wait()

            def step(j, carry):
                multiply(k, pl.ds(pl.multiple_of(j * wide, 128), wide))
                return carry

            lax.fori_loop(0, whole // wide, step, 0)
            if whole < depth:
                multiply(k, slice(whole, depth))
            store(k).start()
            return carry

        lax.fori_loop(0, 2, tile, 0)
        lent["gradient"] = [store(k).wait for k in range(2)]

    def own_step(t):
        own[t].start()
        own_z(t)
        to_core(t, xc.at[t], z)

    def activate_step(t):
        activate(t)
        spread_dpre(t)
        if t == 1:
            own_mixed()
            send(stv.at[b], stv.at[b], st_s.at[0], st_r.at[0], to_x)
            send(stv.at[b], stv.at[b], st_s.at[1], st_r.at[1], to_y)
            send(stv.at[b], stv.at[b], st_s.at[2], st_r.at[2], to_d)

    def core_step(t):
        give_back("core")
        core_terms(t)

    ready = []

    def nearest(j):
        return [z, z + 1 - 2 * (z % 2), 2 - z // 2, 3 * (1 - z // 2)][j]

    def gradient_step(t, j):
        corner = (t, j) not in CORNER_LATER
        if t not in ready:
            ready.append(t)
            all_dpre(t)
        all_pieces(t, nearest(j), corner)
        gradient(t, nearest(j), corner)

    for copy in load_pool:
        copy.start()
    load_w.start()
    pack()
    for t in range(TASKS):
        pre[t] = jnp.broadcast_to(bias[t:t + 1, :], (rows, cols))
    ends = LAYERS - 1
    pl.semaphore_wait(barrier, 4 + (z + ends - 1) // ends + (2 * ends - 1 - z) // ends)
    steps = {
        "places": places, "own": own_step, "layer": z_step, "share": square_sends, "forward": forward,
        "activate": activate_step, "core_terms": core_step, "chain": chain_step, "square": square_step,
        "corner": corner_step, "dpre": forward_dpre, "mixed": mixed_step, "gradient": gradient_step,
    }
    loaded = False
    for name, *which in ORDER:
        if name == "forward" and not loaded:
            load_w.wait()
            loaded = True
        steps[name](*which)
    for t, j in CORNER_LATER:
        corner_pieces(t, nearest(j))
    for layer in range(LAYERS):
        arrived(mg.at[layer * 2 + 1 - c], mc_r.at[layer])
    arrived(stv.at[bx], st_r.at[0])
    arrived(stv.at[by], st_r.at[1])
    arrived(stv.at[bd], st_r.at[2])
    for name in list(lent):
        give_back(name)
    for drain in drains:
        drain()
    st[...] = stv[...]
    at[0] = z // (LAYERS // 2)
    at[1] = bd
    at[2] = (jnp.max(stv[:, 6, :]) > rows).astype(jnp.int32)


def run_exchange(pool_in, weights, bias, stitch, crops, mask, first, cotangent, rows):
    tasks, slots, depth = pool_in.shape
    cols = weights.shape[2]
    parts = weights.shape[1] // depth
    sem = pltpu.SemaphoreType.DMA
    any_spec = pl.BlockSpec(memory_space=pl.ANY)
    vmem_spec = pl.BlockSpec(memory_space=pltpu.VMEM)
    two, four = TASKS, LAYERS
    piece = (rows, depth)
    return pl.pallas_call(
        exchange,
        out_shape=(
            jax.ShapeDtypeStruct((parts, tasks, GROUP * rows, depth), BF16),
            jax.ShapeDtypeStruct((tasks, GROUP * rows, cols), BF16),
            jax.ShapeDtypeStruct((parts, tasks, rows, cols), BF16),
            jax.ShapeDtypeStruct((tasks, rows, depth), BF16),
            jax.ShapeDtypeStruct((GROUP, 8, cols), F32),
            jax.ShapeDtypeStruct((slots, rows), BF16),
            jax.ShapeDtypeStruct((tasks, parts, cols, depth), BF16),
            jax.ShapeDtypeStruct((3,), jnp.int32),
        ),
        in_specs=[any_spec, any_spec] + [vmem_spec] * 6,
        out_specs=(any_spec, any_spec, any_spec, any_spec, vmem_spec, vmem_spec, any_spec, pl.BlockSpec(memory_space=pltpu.SMEM)),
        scratch_shapes=[
            pltpu.VMEM(weights.shape, BF16),
            pltpu.VMEM((tasks, rows, cols), F32),
            pltpu.VMEM((tasks, rows, cols), BF16),
            pltpu.VMEM((tasks, rows, cols), BF16),
            pltpu.VMEM((2, GROUP * rows, depth), BF16),
            pltpu.VMEM((tasks, *piece), BF16),
            pltpu.VMEM((tasks, rows, cols), BF16),
            pltpu.VMEM((GROUP * rows, cols), BF16),
            pltpu.VMEM((cols, GROUP * rows), BF16),
            pltpu.VMEM((2, cols, depth), BF16),
            pltpu.VMEM((rows, 1), F32),
            pltpu.VMEM((rows, depth // 3), F32),
            pltpu.VMEM((LAYERS, *piece), BF16),
            pltpu.VMEM((tasks, LAYERS - 1, *piece), BF16),
            pltpu.VMEM((tasks, LAYERS - 1, *piece), BF16),
            pltpu.VMEM((LAYERS, *piece), BF16),
            pltpu.VMEM((tasks, LAYERS, *piece), BF16),
            pltpu.VMEM((GROUP, 8, cols), F32),
            sem, sem((2 * GROUP,)), sem((two,)),
            sem((two, four)), sem((two, four)), sem((two, four)),
            sem((two, four)), sem((two, four)), sem((two, four)), sem((two, four)), sem((two, four)),
            sem((two, four)), sem((4, two, four)), sem((4, two, four)),
            sem((two, 4)), sem((two, 3)),
            sem((four,)), sem((four,)), sem((four,)), sem((four,)), sem((four + 1,)),
            sem((two, four)), sem((two, four)), sem((two, four)), sem((two, four)), sem((two, four)),
            sem((3,)), sem((3,)), sem((two,)), sem((2,)), sem((two, four)), sem((two, four)), sem((two, four)), sem((two, four)),
        ],
        compiler_params=pltpu.CompilerParams(
            collective_id=0, has_side_effects=True, vmem_limit_bytes=60 * 1024 * 1024),
        cost_estimate=pl.CostEstimate(
            flops=8 * tasks * rows * parts * depth * cols, bytes_accessed=150_000_000, transcendentals=0),
    )(pool_in, weights, bias, stitch, crops, mask, first, cotangent)


def block_of(p, at):
    half = pl.num_programs(0) // 2
    return p // 2 + half * ((at[0] + p % 2) % 2)


def finish(count, at, *refs):
    ins, (mixed, input_grad, weight_grad, bias_grad, stitch_grad, eye) = refs[:8 * count], refs[8 * count:]
    late = pl.program_id(0) % 2 == 1
    side = eye.shape[0]

    @pl.when(pl.program_id(0) == 0)
    def _():
        same = lax.broadcasted_iota(jnp.int32, eye.shape, 0) == lax.broadcasted_iota(jnp.int32, eye.shape, 1)
        eye[...] = jnp.where(same, 1.0, 0.0).astype(BF16)
        small = sum(jnp.sum(ins[8 * k + 7][...], axis=0) for k in range(count))
        bias_grad[...] = small[4:6, :]
        for t in range(TASKS):
            stitch_grad[t] = small[2 * t:2 * t + 2, :]

    for k in range(count):
        xg, dg, mg, ig, place, some, wg, st = ins[8 * k:8 * k + 8]
        depth = wg.shape[3]

        def put(ref, at, value):
            if k == 0:
                ref[at] = value.astype(ref.dtype)
            else:
                ref[at] += value.astype(ref.dtype)

        for t in range(TASKS):
            for low in range(0, depth, side):
                part = slice(low, min(low + side, depth))
                size = part.stop - low
                put(weight_grad, (t, part), lax.dot_general(
                    eye[0:size, 0:size], wg[t, 0, :, part], (((1,), (1,)), ((), ())), preferred_element_type=F32))

        @pl.when(late)
        def _():
            weight_grad[1] += lax.dot_general(
                xg[0, 0], dg[0], (((0,), (0,)), ((), ())), preferred_element_type=F32)

        for t in range(TASKS):
            put(mixed, t, jnp.dot(place[...], mg[0, t], preferred_element_type=F32))
            put(input_grad, t, jnp.dot(some[...], ig[t], preferred_element_type=F32))


def run_finish(passes):
    xg, dg, mg, ig, st, place, wg, at = passes[0]
    slots, rows = place.shape
    parts, tasks, all_rows, depth = xg.shape
    cols = dg.shape[2]
    some = slots // parts
    in_specs = [
        pl.BlockSpec((1, 1, rows, depth), lambda p, at: (p // 2 + parts // 2 * ((at[0] + 1) % 2), 1, at[1], 0)),
        pl.BlockSpec((1, rows, cols), lambda p, at: (1, at[1], 0)),
        pl.BlockSpec((1, tasks, rows, cols), lambda p, at: (block_of(p, at), 0, 0, 0)),
        pl.BlockSpec((tasks, rows, depth), lambda p, at: (0, 0, 0)),
        pl.BlockSpec((slots, rows), lambda p, at: (0, 0)),
        pl.BlockSpec((some, rows), lambda p, at: (p, 0)),
        pl.BlockSpec((tasks, 1, cols, depth), lambda p, at: (0, block_of(p, at), 0, 0)),
        pl.BlockSpec(st.shape, lambda p, at: (0, 0, 0)),
    ]
    flops = 2 * tasks * parts * cols * (rows * depth // 4 + slots * rows)
    return pl.pallas_call(
        functools.partial(finish, len(passes)),
        grid_spec=pltpu.PrefetchScalarGridSpec(
            num_scalar_prefetch=1,
            grid=(parts,),
            in_specs=in_specs * len(passes),
            out_specs=(
                pl.BlockSpec((tasks, slots, cols), lambda p, at: (0, 0, block_of(p, at))),
                pl.BlockSpec((tasks, some, depth), lambda p, at: (0, p, 0)),
                pl.BlockSpec((tasks, depth, cols), lambda p, at: (0, block_of(p, at), 0)),
                pl.BlockSpec((tasks, cols), lambda p, at: (0, 0)),
                pl.BlockSpec((tasks, tasks, cols), lambda p, at: (0, 0, 0)),
            ),
            scratch_shapes=[pltpu.VMEM((256, 256), BF16)],
        ),
        out_shape=(
            jax.ShapeDtypeStruct((tasks, slots, parts * cols), BF16),
            jax.ShapeDtypeStruct((tasks, slots, depth), BF16),
            jax.ShapeDtypeStruct((tasks, parts * depth, cols), F32),
            jax.ShapeDtypeStruct((tasks, cols), F32),
            jax.ShapeDtypeStruct((tasks, tasks, cols), F32),
        ),
        compiler_params=pltpu.CompilerParams(vmem_limit_bytes=60 * 1024 * 1024),
        cost_estimate=pl.CostEstimate(flops=flops, bytes_accessed=75_000_000, transcendentals=0),
    )(at, *[v for out in passes for v in (*out[:4], out[5], out[5], out[6], out[4])])


def packed_body(pool_in, weights, bias, stitch, crops, row_mask, cotangent):
    slots = row_mask.shape[0]
    rows = (slots * 17 // 32 + 15) // 16 * 16

    def part(first):
        return run_exchange(pool_in, weights, bias, stitch, crops.reshape(1, -1), row_mask.reshape(1, -1),
                            jnp.full((1, 1), first, jnp.int32), cotangent, rows)

    front = part(0)
    more = front[7][2] > 0
    return lax.cond(more, lambda: run_finish([front, part(rows)]), lambda: run_finish([front]))


def plain_body(pool_in, weights, bias, stitch, crops, row_mask, cotangent):
    hp = lax.Precision.HIGHEST
    count, valid = row_weights(crops, row_mask)
    features = lax.all_gather(pool_in, "mp", axis=2, tiled=True)
    linear = jnp.einsum("trk,tkc->trc", features, weights, preferred_element_type=jnp.float32)
    pre = linear + bias[:, None, :]
    hidden, gelu_back = jax.vjp(jax.nn.gelu, pre)
    stitched = stitch[:, 0, None, :] * hidden[0][None] + stitch[:, 1, None, :] * hidden[1][None]
    local_mixed = (valid[None, :, None] * stitched).astype(jnp.bfloat16)
    mixed = lax.all_gather(local_mixed, "mp", axis=2, tiled=True)
    scaled = valid[None, :, None] * cotangent.astype(jnp.float32) / count[None, :, None]
    stitch_part = jnp.einsum("trc,urc->tuc", scaled, hidden, precision=hp)
    through = jnp.einsum("tuc,trc->urc", stitch, scaled, precision=hp)
    dpre = gelu_back(through)[0].astype(jnp.bfloat16)
    bias_part = jnp.sum(dpre.astype(jnp.float32), axis=1)
    weight_part = jnp.einsum("trk,trc->tkc", features, dpre, preferred_element_type=jnp.float32)
    terms = jnp.einsum("trc,tkc->trk", dpre, weights, preferred_element_type=jnp.float32)
    input_sum = lax.psum_scatter(terms, "mp", scatter_dimension=2, tiled=True)
    weight_grad, bias_grad, stitch_grad = lax.psum((weight_part, bias_part, stitch_part), "batch")
    return (mixed, input_sum.astype(jnp.bfloat16), weight_grad, bias_grad, stitch_grad)


def solution(mesh):
    square = mesh.shape["batch"] == GROUP and mesh.shape["mp"] == 2 * LAYERS
    return jax.shard_map(
        packed_body if square else plain_body,
        mesh=mesh,
        in_specs=(
            P(None, "batch", "mp"),
            P(None, None, "mp"),
            P(None, "mp"),
            P(None, None, "mp"),
            P("batch"),
            P("batch"),
            P(None, "batch", "mp"),
        ),
        out_specs=(
            P(None, "batch", None),
            P(None, "batch", "mp"),
            P(None, None, "mp"),
            P(None, "mp"),
            P(None, None, "mp"),
        ),
        check_vma=False,
    )
```

```python
import functools

import jax
import jax.numpy as jnp
from jax import lax
from jax.experimental import pallas as pl
from jax.experimental.pallas import tpu as pltpu
from jax.sharding import PartitionSpec as P

MESH = pl.DeviceIdType.MESH
F32 = jnp.float32
BF16 = jnp.bfloat16
LAYERS = 4
GROUP = 4
TASKS = 2
TANH_SCALE = 0.7978845608
TANH_CUBE = 0.044715

CORNER_LATER = ((1, 2), (1, 3))
HALVED = ()
VIA_LAYERS = ((0, 0), (0, 3))
ORDER = (
    ("share", 0, 0), ("own", 0), ("share", 1, 0), ("layer", 0, 1), ("square", 0, 0), ("share", 0, 1), ("layer", 0, 2),
    ("forward", 0, 0), ("share", 0, 2), ("own", 1), ("forward", 0, 1), ("layer", 0, 3), ("forward", 0, 2),
    ("corner", 0, 0), ("forward", 0, 3), ("activate", 0), ("core_terms", 0), ("layer", 1, 1), ("square", 0, 1),
    ("square", 1, 0), ("chain", 0, 0), ("layer", 1, 2), ("square", 0, 2), ("forward", 1, 2), ("forward", 1, 1),
    ("chain", 0, 1), ("dpre", 0), ("corner", 0, 1), ("share", 1, 1), ("chain", 0, 2), ("forward", 1, 0),
    ("layer", 1, 3), ("share", 0, 3), ("forward", 1, 3), ("activate", 1), ("gradient", 0, 1), ("corner", 0, 2),
    ("share", 1, 2), ("chain", 0, 3), ("core_terms", 1), ("gradient", 0, 0), ("chain", 1, 0), ("mixed", 1),
    ("gradient", 0, 2), ("dpre", 1), ("corner", 1, 0), ("square", 0, 3), ("corner", 0, 3), ("places",),
    ("share", 1, 3), ("square", 1, 1), ("gradient", 0, 3), ("chain", 1, 1), ("square", 1, 2), ("gradient", 1, 0),
    ("square", 1, 3), ("chain", 1, 2), ("mixed", 2), ("gradient", 1, 2), ("gradient", 1, 3), ("corner", 1, 1),
    ("corner", 1, 2), ("chain", 1, 3), ("gradient", 1, 1), ("mixed", 3), ("corner", 1, 3),
)


def row_weights(crops, row_mask):
    slots = jnp.arange(row_mask.shape[0], dtype=jnp.int32)
    ends = jnp.cumsum(crops)
    image = jnp.sum((slots[:, None] >= ends[None, :]).astype(jnp.int32), axis=1)
    inside = slots < ends[-1]
    onehot = (image[:, None] == jnp.arange(crops.shape[0], dtype=jnp.int32)[None, :]).astype(
        jnp.int32
    )
    count = jnp.sum(onehot * crops[None, :], axis=1)
    count = jnp.where(inside, count, 1).astype(jnp.float32)
    valid = (row_mask * inside.astype(jnp.int32)).astype(jnp.float32)
    return (count, valid)


def exchange(pool, w, bias, stitch, crops, mask, first, cotangent, xg, dg, mg, ig, st, place, wg, at,
             wv, pre, dpv, mxv, gx, xc, cot, picked, dgv, dgt, gout, scale, acc, sbuf, rup, rdn, tso, tsi, stv,
             wsem, lsem, osem, z_r, z_u, z_d, o_x, o_y, r_x, r_y, r_d, f_s, c_r, c_s,
             dp_s, dp_r, m_r, m_u, m_d, mc_r, mc_s, t_u, t_d, t_s, tc_r, tc_s, st_s, st_r, ig_s, go_s, v_u, v_d, f_h, r_h):
    rows, depth = xc.shape[1], xc.shape[2]
    cols, slots, images = w.shape[2], mask.shape[1], crops.shape[1]
    b, m = lax.axis_index("batch"), lax.axis_index("mp")
    z, c = m // 2, m % 2
    y, x = b // 2, b % 2
    bx, by, bd = y * 2 + (1 - x), (1 - y) * 2 + x, 3 - b
    to_x, to_y, to_d = (bx, m), (by, m), (bd, m)
    to_c = (b, z * 2 + 1 - c)
    up, down = (b, m + 2), (b, m - 2)
    not_top, not_bottom = z < LAYERS - 1, z > 0
    everyone = [(None, to_x), (None, to_y), (None, to_d), (None, to_c), (not_top, up), (not_bottom, down)]

    barrier = pltpu.get_barrier_semaphore()
    for cond, dev in everyone:
        def greet(dev=dev):
            pl.semaphore_signal(barrier, inc=1, device_id=dev, device_id_type=MESH)
        greet() if cond is None else pl.when(cond)(greet)
    drains = []
    lent = {}

    def give_back(name):
        for drain in lent.pop(name, ()):
            drain()

    def remote(src, dst, send, recv, dev):
        return pltpu.make_async_remote_copy(
            src_ref=src, dst_ref=dst, send_sem=send, recv_sem=recv, device_id=dev, device_id_type=MESH)

    def send(src, dst, ssem, rsem, dev, cond=None):
        def go():
            remote(src, dst, ssem, rsem, dev).start()
        def drain():
            remote(src, dst, ssem, rsem, dev).wait_send()
        if cond is None:
            go()
            drains.append(drain)
        else:
            pl.when(cond)(go)
            drains.append(lambda: pl.when(cond)(drain))

    def arrived(dst, rsem, cond=None):
        def go():
            remote(dst, dst, rsem, rsem, to_c).wait_recv()
        go() if cond is None else pl.when(cond)(go)

    def local(src, dst, sem):
        copy = pltpu.make_async_copy(src, dst, sem)
        copy.start()
        drains.append(copy.wait)
        return copy

    def span(who):
        return pl.ds(pl.multiple_of(who * rows, 16), rows)

    top = (rows // 2 + 15) // 16 * 16
    outer = (z == 0) | (z == LAYERS - 1)
    inner = jnp.logical_not(outer)

    def slot(t, layer, plane, who, half=None):
        part = span(who)
        if half is not None:
            part = pl.ds(pl.multiple_of(who * rows + half * top, 16), rows - top if half else top)
        return xg.at[layer * 2 + plane, t, part, :]

    load_w = pltpu.make_async_copy(w, wv, wsem)
    load_pool = [pltpu.make_async_copy(pool.at[t], gx.at[t, pl.ds(0, slots), :], lsem.at[t]) for t in range(TASKS)]

    def grid(shape, axis):
        return lax.broadcasted_iota(jnp.int32, shape, axis).astype(F32)

    def row_weights():
        square = (images, images)
        wide = jnp.broadcast_to(crops[...].astype(F32), square)
        lane, sub = grid(square, 1), grid(square, 0)
        end = jnp.sum(jnp.where(lane <= sub, wide, 0.0), axis=1, keepdims=True)
        crop = jnp.sum(jnp.where(lane == sub, wide, 0.0), axis=1, keepdims=True)
        at = grid((images, slots), 1)
        inside = jnp.where((at < end) & (at >= end - crop), 1.0, 0.0)
        count = jnp.sum(inside * crop, axis=0, keepdims=True)
        valid = mask[...].astype(F32) * jnp.sum(inside, axis=0, keepdims=True)
        return valid, valid / jnp.maximum(count, 1.0)

    def pack():
        valid, weight = row_weights()
        square = (slots, slots)
        upto = jnp.where(grid(square, 0) <= grid(square, 1), 1.0, 0.0).astype(BF16)
        many = jnp.broadcast_to(valid, (16, slots)).astype(BF16)
        index = jnp.dot(many, upto, preferred_element_type=F32)[0:1, :] - 1.0 - first[...].astype(F32)
        pick = jnp.where((grid((rows, slots), 0) == index) & (valid > 0.0), 1.0, 0.0)
        scale[...] = jnp.sum(pick * weight, axis=1, keepdims=True)
        stv[b, 6:7, :] = jnp.broadcast_to(jnp.sum(valid, axis=1, keepdims=True), (1, cols))
        stv[b, 7:8, :] = jnp.zeros((1, cols), F32)
        pick = pick.astype(BF16)
        picked[...] = pick
        pack_task(0)

    def pack_task(t):
        load_pool[t].wait()
        xc[t] = jnp.dot(picked[...], gx[t, 0:slots, :], preferred_element_type=F32).astype(BF16)

    def pack_rest():
        pack_task(1)
        for t in range(TASKS):
            cot[t] = jnp.dot(picked[...], cotangent[t], preferred_element_type=F32).astype(BF16)
            pre[t] = jnp.broadcast_to(bias[t:t + 1, :], (rows, cols))

    def places():
        valid, _ = row_weights()
        square = (slots, slots)
        wide = jnp.broadcast_to(valid, square)
        lane, sub = grid(square, 1), grid(square, 0)
        index = jnp.sum(jnp.where(lane <= sub, wide, 0.0), axis=1, keepdims=True) - 1.0 - first[...].astype(F32)
        here = jnp.sum(jnp.where(lane == sub, wide, 0.0), axis=1, keepdims=True)
        place[...] = jnp.where((grid((slots, rows), 1) == index) & (here > 0.0), 1.0, 0.0).astype(BF16)

    own = [pltpu.make_async_copy(xc.at[t], slot(t, z, c, b), osem.at[t]) for t in range(TASKS)]

    def own_z(t):
        send(xc.at[t], slot(t, z, c, b), z_u.at[t, z], z_r.at[t, z], up, not_top)
        send(xc.at[t], slot(t, z, c, b), z_d.at[t, z], z_r.at[t, z], down, not_bottom)

    def to_core(t, src, layer, cond=None):
        send(src, slot(t, layer, c, b), c_s.at[0, t, layer], c_r.at[0, t, layer], to_c, cond)

    def to_square(t, src, layer, cond=None):
        send(src, slot(t, layer, c, b), o_x.at[t, layer], r_x.at[t, layer], to_x, cond)
        send(src, slot(t, layer, c, b), o_y.at[t, layer], r_y.at[t, layer], to_y, cond)

    def near(d):
        return [(z, None)] if d == 0 else [(z - d, z >= d), (z + d, z < LAYERS - d)]

    def z_step(t, d):
        (low, is_low), (high, is_high) = near(d)
        here = slot(t, low, c, b)
        arrived(here, z_r.at[t, low], is_low)
        send(here, here, z_u.at[t, low], z_r.at[t, low], up, is_low & not_top)
        to_core(t, here, low, is_low)
        there = slot(t, high, c, b)
        arrived(there, z_r.at[t, high], is_high)
        send(there, there, z_d.at[t, high], z_r.at[t, high], down, is_high & not_bottom)
        to_core(t, there, high, is_high)

    def square_sends(t, d):
        for layer, cond in near(d):
            to_square(t, xc.at[t] if d == 0 else slot(t, layer, c, b), layer, cond)

    def via_layers(t, layer):
        hit = [layer == chosen for task, chosen in VIA_LAYERS if task == t]
        return functools.reduce(lambda p, q: p | q, hit) if hit else None

    def square_step(t, d):
        for layer, cond in near(d):
            from_x, from_y = slot(t, layer, c, bx), slot(t, layer, c, by)
            even, odd = (t + layer) % 2 == 0, (t + layer) % 2 == 1
            if cond is not None:
                even, odd = even & cond, odd & cond
            if d > 0 and via_layers(t, layer) is not None:
                around = jnp.logical_not(via_layers(t, layer))
                even, odd = even & around, odd & around
            halved = (t, d) in HALVED
            if halved:
                even, odd = even & inner, odd & inner
            arrived(from_x, r_x.at[t, layer], cond)
            send(from_x, from_x, f_s.at[t, layer], r_d.at[t, layer], to_y, even)
            if halved:
                first = slot(t, layer, c, bx, 0)
                send(first, first, f_s.at[t, layer], r_d.at[t, layer], to_y, cond & outer)
            send(from_x, from_x, c_s.at[1, t, layer], c_r.at[1, t, layer], to_c, cond)
            arrived(from_y, r_y.at[t, layer], cond)
            send(from_y, from_y, f_s.at[t, layer], r_d.at[t, layer], to_x, odd)
            if halved:
                second = slot(t, layer, c, by, 1)
                send(second, second, f_h.at[t, layer], r_h.at[t, layer], to_x, cond & outer)
            send(from_y, from_y, c_s.at[2, t, layer], c_r.at[2, t, layer], to_c, cond)

    def corner_step(t, d):
        for layer, cond in near(d):
            from_d = slot(t, layer, c, bd)
            if (t, d) in HALVED:
                arrived(from_d, r_d.at[t, layer], cond & inner)
                arrived(slot(t, layer, c, bd, 0), r_d.at[t, layer], cond & outer)
                arrived(slot(t, layer, c, bd, 1), r_h.at[t, layer], cond & outer)
            else:
                arrived(from_d, r_d.at[t, layer], cond)
            on = via_layers(t, layer)
            if on is not None:
                send(from_d, from_d, v_u.at[t, layer], r_d.at[t, layer], up, on & (layer <= z) & not_top)
                send(from_d, from_d, v_d.at[t, layer], r_d.at[t, layer], down, on & (layer >= z) & not_bottom)
            send(from_d, from_d, c_s.at[3, t, layer], c_r.at[3, t, layer], to_c, cond)

    around = (b, bx, by, bd)

    def strip(i):
        return pl.ds(i * rows, rows)

    def forward(t, d):
        def add(mm, source):
            part = pl.ds(pl.multiple_of(mm * depth, 128), depth)

            def half(h, carry):
                out = pl.ds(pl.multiple_of(h * (cols // 2), 128), cols // 2)
                pre[t, :, out] += jnp.dot(source[...], wv[t, part, out], preferred_element_type=F32)
                return carry

            lax.fori_loop(0, 2, half, 0)

        def fetch(i, layer, plane):
            return pltpu.make_async_copy(
                xg.at[layer * 2 + plane, t, span(b), :], gx.at[plane, strip(i), :], lsem.at[i * 2 + plane])

        sides = near(d)
        if d == 0:
            own[t].wait()
        for i, (layer, cond) in enumerate(sides):
            def begin(i=i, layer=layer):
                arrived(slot(t, layer, 1 - c, b), c_r.at[0, t, layer])
                for plane in range(2):
                    fetch(i, layer, plane).start()
            begin() if cond is None else pl.when(cond)(begin)

        def block(n, carry):
            i, plane = n // 2, n % 2
            layer = z + (2 * i - 1) * d

            @pl.when((layer >= 0) & (layer < LAYERS))
            def _():
                pltpu.make_async_copy(
                    xg.at[layer * 2 + plane, t, span(b), :], gx.at[plane, pl.ds(pl.multiple_of(i * rows, 16), rows), :],
                    lsem.at[n]).wait()
                add(layer * 2 + plane, gx.at[plane, pl.ds(pl.multiple_of(i * rows, 16), rows), :])

            return carry

        lax.fori_loop(0, 2 * len(sides), block, 0)

    def fold(v):
        return jnp.sum(v.reshape(2, 8, v.shape[1]), axis=0)

    def activate(u):
        def chunk(i, sums):
            s0, s1, bb = sums
            part = pl.ds(pl.multiple_of(i * 16, 16), 16)
            v = pre[u, part, :]
            th = jnp.tanh(TANH_SCALE * (v + TANH_CUBE * (v * v * v)))
            h = 0.5 * v * (1.0 + th)
            slope = 0.5 * (1.0 + th) + 0.5 * v * (1.0 - th * th) * (TANH_SCALE * (1.0 + 3.0 * TANH_CUBE * (v * v)))
            sc = scale[part, :]
            g0 = cot[0, part, :].astype(F32) * sc
            g1 = cot[1, part, :].astype(F32) * sc
            dpre = (slope * (stitch[0, u:u + 1, :] * g0 + stitch[1, u:u + 1, :] * g1)).astype(BF16)
            dpv[u, part, :] = dpre
            if u == 0:
                pre[0, part, :] = h
            else:
                h0 = pre[0, part, :]
                for t in range(TASKS):
                    mxv[t, part, :] = (stitch[t, 0:1, :] * h0 + stitch[t, 1:2, :] * h).astype(BF16)
            return s0 + fold(g0 * h), s1 + fold(g1 * h), bb + fold(dpre.astype(F32))

        zero = jnp.zeros((8, cols), F32)
        s0, s1, bb = lax.fori_loop(0, rows // 16, chunk, (zero, zero, zero))
        stv[b, u:u + 1, :] = jnp.sum(s0, axis=0, keepdims=True)
        stv[b, 2 + u:3 + u, :] = jnp.sum(s1, axis=0, keepdims=True)
        stv[b, 4 + u:5 + u, :] = jnp.sum(bb, axis=0, keepdims=True)

    def spread_dpre(t):
        mine = dg.at[t, span(b), :]
        pltpu.make_async_copy(dpv.at[t], mine, dp_s.at[t, 3]).start()
        send(dpv.at[t], mine, dp_s.at[t, 0], dp_r.at[t, 0], to_x)
        send(dpv.at[t], mine, dp_s.at[t, 1], dp_r.at[t, 1], to_y)

    def forward_dpre(t):
        from_x, from_y = dg.at[t, span(bx), :], dg.at[t, span(by), :]
        arrived(from_x, dp_r.at[t, 0])
        arrived(from_y, dp_r.at[t, 1])
        if t == 0:
            send(from_x, from_x, dp_s.at[t, 2], dp_r.at[t, 2], to_y)
        else:
            send(from_y, from_y, dp_s.at[t, 2], dp_r.at[t, 2], to_x)

    def own_mixed():
        local(mxv, mg.at[m], mc_s.at[LAYERS])
        send(mxv, mg.at[m], m_u.at[z], m_r.at[z], up, not_top)
        send(mxv, mg.at[m], m_d.at[z], m_r.at[z], down, not_bottom)
        send(mxv, mg.at[m], mc_s.at[z], mc_r.at[z], to_c)

    def mixed_step(d):
        low, high = z - d, z + d
        here = mg.at[low * 2 + c]
        arrived(here, m_r.at[low], z >= d)
        send(here, here, m_u.at[low], m_r.at[low], up, (z >= d) & not_top)
        send(here, here, mc_s.at[low], mc_r.at[low], to_c, z >= d)
        there = mg.at[high * 2 + c]
        arrived(there, m_r.at[high], z < LAYERS - d)
        send(there, there, m_d.at[high], m_r.at[high], down, (z < LAYERS - d) & not_bottom)
        send(there, there, mc_s.at[high], mc_r.at[high], to_c, z < LAYERS - d)

    tiles = 3
    width = depth // tiles

    def lanes(j):
        return pl.ds(pl.multiple_of(j * width, 128), width)

    def term(t, mm, j):
        part = pl.ds(pl.multiple_of(mm * depth + j * width, 128), width)
        return lax.dot_general(dpv[t], wv[t, part, :], (((1,), (1,)), ((), ())), preferred_element_type=F32)

    def core_terms(t):
        def step(s, carry):
            part = pl.ds(pl.multiple_of((2 * s + 1 - c) * depth, 128), depth)
            tso[s] = lax.dot_general(
                dpv[t], wv[t, part, :], (((1,), (1,)), ((), ())), preferred_element_type=F32).astype(BF16)
            remote(tso.at[s], tsi.at[t, s], tc_s.at[t, s], tc_r.at[t, s], to_c).start()
            return carry

        lax.fori_loop(0, LAYERS, step, 0)
        lent["core"] = [lambda s=s: remote(
            tso.at[s], tsi.at[t, s], tc_s.at[t, s], tc_r.at[t, s], to_c).wait_send() for s in range(LAYERS)]

    def chain_step(t, k):
        s = [3 * (1 - z // 2), (2 + 3 * z) % 5, 1 + z % 2, z][k]
        has_up = (s >= z) & not_bottom
        has_down = (s <= z) & not_top
        give_back(k)
        arrived(tsi.at[t, s], tc_r.at[t, s])
        arrived(rup.at[t, s - 1], t_u.at[t, s], has_up)
        arrived(rdn.at[t, s], t_d.at[t, s], has_down)

        def step(j, carry):
            acc[...] = term(t, 2 * s + c, j) + tsi[t, s, :, lanes(j)].astype(F32)

            @pl.when(has_up)
            def _():
                acc[...] += rup[t, s - 1, :, lanes(j)].astype(F32)

            @pl.when(has_down)
            def _():
                acc[...] += rdn[t, s, :, lanes(j)].astype(F32)

            sbuf[s, :, lanes(j)] = acc[...].astype(BF16)
            return carry

        lax.fori_loop(0, tiles, step, 0)
        before = len(drains)
        if k < LAYERS - 1:
            send(sbuf.at[s], rup.at[t, s - 1], t_s.at[t, s], t_u.at[t, s], up, s > z)
            send(sbuf.at[s], rdn.at[t, s], t_s.at[t, s], t_d.at[t, s], down, s < z)
        else:
            local(sbuf.at[s], ig.at[t], ig_s.at[t])
        lent[k] = drains[before:]
        del drains[before:]

    def all_dpre(t):
        arrived(dg.at[t, span(bd), :], dp_r.at[t, 2])
        pltpu.make_async_copy(dpv.at[t], dg.at[t, span(b), :], dp_s.at[t, 3]).wait()
        loads = [pltpu.make_async_copy(dg.at[t, span(who), :], dgv.at[strip(i), :], lsem.at[i])
                 for i, who in enumerate(around)]
        for copy in loads:
            copy.start()
        for copy in loads:
            copy.wait()
        dgt[...] = dgv[...].T

    def all_pieces(t, layer, corner=True):
        for k, who in ((1, bx), (2, by), (3, bd)):
            if k < 3 or corner:
                arrived(slot(t, layer, 1 - c, who), c_r.at[k, t, layer])

    def corner_pieces(t, layer):
        arrived(slot(t, layer, 1 - c, bd), c_r.at[3, t, layer])

    def gradient(t, layer, corner):
        many = GROUP if corner else GROUP - 1

        def load(k):
            mm = 2 * layer + k
            return [pltpu.make_async_copy(xg.at[mm, t, span(who), :], gx.at[k, strip(i), :], lsem.at[k * GROUP + i])
                    for i, who in enumerate(around[:many])]

        def store(k):
            return pltpu.make_async_copy(gout.at[k], wg.at[t, 2 * layer + k], go_s.at[k])

        for k in range(2):
            for copy in load(k):
                copy.start()
        give_back("gradient")
        wide = 2 * 128
        whole = depth // wide * wide

        def multiply(k, part):
            gout[k, :, part] = jnp.dot(
                dgt[:, 0:many * rows], gx[k, 0:many * rows, part], preferred_element_type=F32).astype(BF16)

        def tile(k, carry):
            for i in range(many):
                pltpu.make_async_copy(
                    xg.at[2 * layer + k, t, span(around[i]), :], gx.at[k, strip(i), :], lsem.at[k * GROUP + i]).wait()

            def step(j, carry):
                multiply(k, pl.ds(pl.multiple_of(j * wide, 128), wide))
                return carry

            lax.fori_loop(0, whole // wide, step, 0)
            if whole < depth:
                multiply(k, slice(whole, depth))
            store(k).start()
            return carry

        lax.fori_loop(0, 2, tile, 0)
        lent["gradient"] = [store(k).wait for k in range(2)]

    def own_step(t):
        own[t].start()
        own_z(t)
        to_core(t, xc.at[t], z)

    def activate_step(t):
        activate(t)
        spread_dpre(t)
        if t == 1:
            own_mixed()
            send(stv.at[b], stv.at[b], st_s.at[0], st_r.at[0], to_x)
            send(stv.at[b], stv.at[b], st_s.at[1], st_r.at[1], to_y)
            send(stv.at[b], stv.at[b], st_s.at[2], st_r.at[2], to_d)

    def core_step(t):
        give_back("core")
        core_terms(t)

    ready = []

    def nearest(j):
        return [z, z + 1 - 2 * (z % 2), 2 - z // 2, 3 * (1 - z // 2)][j]

    def gradient_step(t, j):
        corner = (t, j) not in CORNER_LATER
        if t not in ready:
            ready.append(t)
            all_dpre(t)
        all_pieces(t, nearest(j), corner)
        gradient(t, nearest(j), corner)

    for copy in load_pool:
        copy.start()
    load_w.start()
    pack()
    ends = LAYERS - 1
    pl.semaphore_wait(barrier, 4 + (z + ends - 1) // ends + (2 * ends - 1 - z) // ends)
    steps = {
        "places": places, "own": own_step, "layer": z_step, "share": square_sends, "forward": forward,
        "activate": activate_step, "core_terms": core_step, "chain": chain_step, "square": square_step,
        "corner": corner_step, "dpre": forward_dpre, "mixed": mixed_step, "gradient": gradient_step,
    }
    loaded = packed = False
    for name, *which in ORDER:
        if not packed and (name, *which) not in (("own", 0), ("share", 0, 0)):
            pack_rest()
            packed = True
        if name == "forward" and not loaded:
            load_w.wait()
            loaded = True
        steps[name](*which)
    for t, j in CORNER_LATER:
        corner_pieces(t, nearest(j))
    for layer in range(LAYERS):
        arrived(mg.at[layer * 2 + 1 - c], mc_r.at[layer])
    arrived(stv.at[bx], st_r.at[0])
    arrived(stv.at[by], st_r.at[1])
    arrived(stv.at[bd], st_r.at[2])
    for name in list(lent):
        give_back(name)
    for drain in drains:
        drain()
    st[...] = stv[...]
    at[0] = z // (LAYERS // 2)
    at[1] = bd
    at[2] = (jnp.max(stv[:, 6, :]) > rows).astype(jnp.int32)


def run_exchange(pool_in, weights, bias, stitch, crops, mask, first, cotangent, rows):
    tasks, slots, depth = pool_in.shape
    cols = weights.shape[2]
    parts = weights.shape[1] // depth
    sem = pltpu.SemaphoreType.DMA
    any_spec = pl.BlockSpec(memory_space=pl.ANY)
    vmem_spec = pl.BlockSpec(memory_space=pltpu.VMEM)
    two, four = TASKS, LAYERS
    piece = (rows, depth)
    return pl.pallas_call(
        exchange,
        out_shape=(
            jax.ShapeDtypeStruct((parts, tasks, GROUP * rows, depth), BF16),
            jax.ShapeDtypeStruct((tasks, GROUP * rows, cols), BF16),
            jax.ShapeDtypeStruct((parts, tasks, rows, cols), BF16),
            jax.ShapeDtypeStruct((tasks, rows, depth), BF16),
            jax.ShapeDtypeStruct((GROUP, 8, cols), F32),
            jax.ShapeDtypeStruct((slots, rows), BF16),
            jax.ShapeDtypeStruct((tasks, parts, cols, depth), BF16),
            jax.ShapeDtypeStruct((3,), jnp.int32),
        ),
        in_specs=[any_spec, any_spec] + [vmem_spec] * 6,
        out_specs=(any_spec, any_spec, any_spec, any_spec, vmem_spec, vmem_spec, any_spec, pl.BlockSpec(memory_space=pltpu.SMEM)),
        scratch_shapes=[
            pltpu.VMEM(weights.shape, BF16),
            pltpu.VMEM((tasks, rows, cols), F32),
            pltpu.VMEM((tasks, rows, cols), BF16),
            pltpu.VMEM((tasks, rows, cols), BF16),
            pltpu.VMEM((2, GROUP * rows, depth), BF16),
            pltpu.VMEM((tasks, *piece), BF16),
            pltpu.VMEM((tasks, rows, cols), BF16),
            pltpu.VMEM((rows, slots), BF16),
            pltpu.VMEM((GROUP * rows, cols), BF16),
            pltpu.VMEM((cols, GROUP * rows), BF16),
            pltpu.VMEM((2, cols, depth), BF16),
            pltpu.VMEM((rows, 1), F32),
            pltpu.VMEM((rows, depth // 3), F32),
            pltpu.VMEM((LAYERS, *piece), BF16),
            pltpu.VMEM((tasks, LAYERS - 1, *piece), BF16),
            pltpu.VMEM((tasks, LAYERS - 1, *piece), BF16),
            pltpu.VMEM((LAYERS, *piece), BF16),
            pltpu.VMEM((tasks, LAYERS, *piece), BF16),
            pltpu.VMEM((GROUP, 8, cols), F32),
            sem, sem((2 * GROUP,)), sem((two,)),
            sem((two, four)), sem((two, four)), sem((two, four)),
            sem((two, four)), sem((two, four)), sem((two, four)), sem((two, four)), sem((two, four)),
            sem((two, four)), sem((4, two, four)), sem((4, two, four)),
            sem((two, 4)), sem((two, 3)),
            sem((four,)), sem((four,)), sem((four,)), sem((four,)), sem((four + 1,)),
            sem((two, four)), sem((two, four)), sem((two, four)), sem((two, four)), sem((two, four)),
            sem((3,)), sem((3,)), sem((two,)), sem((2,)), sem((two, four)), sem((two, four)), sem((two, four)), sem((two, four)),
        ],
        compiler_params=pltpu.CompilerParams(
            collective_id=0, has_side_effects=True, vmem_limit_bytes=60 * 1024 * 1024),
        cost_estimate=pl.CostEstimate(
            flops=8 * tasks * rows * parts * depth * cols, bytes_accessed=150_000_000, transcendentals=0),
    )(pool_in, weights, bias, stitch, crops, mask, first, cotangent)


def block_of(p, at):
    half = pl.num_programs(0) // 2
    return p // 2 + half * ((at[0] + p % 2) % 2)


def finish(count, at, *refs):
    ins, (mixed, input_grad, weight_grad, bias_grad, stitch_grad, eye) = refs[:8 * count], refs[8 * count:]
    late = pl.program_id(0) % 2 == 1
    side = eye.shape[0]

    @pl.when(pl.program_id(0) == 0)
    def _():
        same = lax.broadcasted_iota(jnp.int32, eye.shape, 0) == lax.broadcasted_iota(jnp.int32, eye.shape, 1)
        eye[...] = jnp.where(same, 1.0, 0.0).astype(BF16)
        small = sum(jnp.sum(ins[8 * k + 7][...], axis=0) for k in range(count))
        bias_grad[...] = small[4:6, :]
        for t in range(TASKS):
            stitch_grad[t] = small[2 * t:2 * t + 2, :]

    for k in range(count):
        xg, dg, mg, ig, place, some, wg, st = ins[8 * k:8 * k + 8]
        depth = wg.shape[3]

        def put(ref, at, value):
            if k == 0:
                ref[at] = value.astype(ref.dtype)
            else:
                ref[at] += value.astype(ref.dtype)

        put(weight_grad, 0, wg[0, 0].T.astype(F32))
        for low in range(0, depth, side):
            part = slice(low, min(low + side, depth))
            size = part.stop - low
            put(weight_grad, (1, part), lax.dot_general(
                eye[0:size, 0:size], wg[1, 0, :, part], (((1,), (1,)), ((), ())), preferred_element_type=F32))

        @pl.when(late)
        def _():
            weight_grad[1] += lax.dot_general(
                xg[0, 0], dg[0], (((0,), (0,)), ((), ())), preferred_element_type=F32)

        for t in range(TASKS):
            put(mixed, t, jnp.dot(place[...], mg[0, t], preferred_element_type=F32))
            put(input_grad, t, jnp.dot(some[...], ig[t], preferred_element_type=F32))


def run_finish(passes):
    xg, dg, mg, ig, st, place, wg, at = passes[0]
    slots, rows = place.shape
    parts, tasks, all_rows, depth = xg.shape
    cols = dg.shape[2]
    some = slots // parts
    in_specs = [
        pl.BlockSpec((1, 1, rows, depth), lambda p, at: (p // 2 + parts // 2 * ((at[0] + 1) % 2), 1, at[1], 0)),
        pl.BlockSpec((1, rows, cols), lambda p, at: (1, at[1], 0)),
        pl.BlockSpec((1, tasks, rows, cols), lambda p, at: (block_of(p, at), 0, 0, 0)),
        pl.BlockSpec((tasks, rows, depth), lambda p, at: (0, 0, 0)),
        pl.BlockSpec((slots, rows), lambda p, at: (0, 0)),
        pl.BlockSpec((some, rows), lambda p, at: (p, 0)),
        pl.BlockSpec((tasks, 1, cols, depth), lambda p, at: (0, block_of(p, at), 0, 0)),
        pl.BlockSpec(st.shape, lambda p, at: (0, 0, 0)),
    ]
    flops = 2 * tasks * parts * cols * (rows * depth // 4 + slots * rows)
    return pl.pallas_call(
        functools.partial(finish, len(passes)),
        grid_spec=pltpu.PrefetchScalarGridSpec(
            num_scalar_prefetch=1,
            grid=(parts,),
            in_specs=in_specs * len(passes),
            out_specs=(
                pl.BlockSpec((tasks, slots, cols), lambda p, at: (0, 0, block_of(p, at))),
                pl.BlockSpec((tasks, some, depth), lambda p, at: (0, p, 0)),
                pl.BlockSpec((tasks, depth, cols), lambda p, at: (0, block_of(p, at), 0)),
                pl.BlockSpec((tasks, cols), lambda p, at: (0, 0)),
                pl.BlockSpec((tasks, tasks, cols), lambda p, at: (0, 0, 0)),
            ),
            scratch_shapes=[pltpu.VMEM((256, 256), BF16)],
        ),
        out_shape=(
            jax.ShapeDtypeStruct((tasks, slots, parts * cols), BF16),
            jax.ShapeDtypeStruct((tasks, slots, depth), BF16),
            jax.ShapeDtypeStruct((tasks, parts * depth, cols), F32),
            jax.ShapeDtypeStruct((tasks, cols), F32),
            jax.ShapeDtypeStruct((tasks, tasks, cols), F32),
        ),
        compiler_params=pltpu.CompilerParams(vmem_limit_bytes=60 * 1024 * 1024),
        cost_estimate=pl.CostEstimate(flops=flops, bytes_accessed=75_000_000, transcendentals=0),
    )(at, *[v for out in passes for v in (*out[:4], out[5], out[5], out[6], out[4])])


def packed_body(pool_in, weights, bias, stitch, crops, row_mask, cotangent):
    slots = row_mask.shape[0]
    rows = (slots * 17 // 32 + 15) // 16 * 16

    def part(first):
        return run_exchange(pool_in, weights, bias, stitch, crops.reshape(1, -1), row_mask.reshape(1, -1),
                            jnp.full((1, 1), first, jnp.int32), cotangent, rows)

    front = part(0)
    more = front[7][2] > 0
    return lax.cond(more, lambda: run_finish([front, part(rows)]), lambda: run_finish([front]))


def plain_body(pool_in, weights, bias, stitch, crops, row_mask, cotangent):
    hp = lax.Precision.HIGHEST
    count, valid = row_weights(crops, row_mask)
    features = lax.all_gather(pool_in, "mp", axis=2, tiled=True)
    linear = jnp.einsum("trk,tkc->trc", features, weights, preferred_element_type=jnp.float32)
    pre = linear + bias[:, None, :]
    hidden, gelu_back = jax.vjp(jax.nn.gelu, pre)
    stitched = stitch[:, 0, None, :] * hidden[0][None] + stitch[:, 1, None, :] * hidden[1][None]
    local_mixed = (valid[None, :, None] * stitched).astype(jnp.bfloat16)
    mixed = lax.all_gather(local_mixed, "mp", axis=2, tiled=True)
    scaled = valid[None, :, None] * cotangent.astype(jnp.float32) / count[None, :, None]
    stitch_part = jnp.einsum("trc,urc->tuc", scaled, hidden, precision=hp)
    through = jnp.einsum("tuc,trc->urc", stitch, scaled, precision=hp)
    dpre = gelu_back(through)[0].astype(jnp.bfloat16)
    bias_part = jnp.sum(dpre.astype(jnp.float32), axis=1)
    weight_part = jnp.einsum("trk,trc->tkc", features, dpre, preferred_element_type=jnp.float32)
    terms = jnp.einsum("trc,tkc->trk", dpre, weights, preferred_element_type=jnp.float32)
    input_sum = lax.psum_scatter(terms, "mp", scatter_dimension=2, tiled=True)
    weight_grad, bias_grad, stitch_grad = lax.psum((weight_part, bias_part, stitch_part), "batch")
    return (mixed, input_sum.astype(jnp.bfloat16), weight_grad, bias_grad, stitch_grad)


def solution(mesh):
    square = mesh.shape["batch"] == GROUP and mesh.shape["mp"] == 2 * LAYERS
    return jax.shard_map(
        packed_body if square else plain_body,
        mesh=mesh,
        in_specs=(
            P(None, "batch", "mp"),
            P(None, None, "mp"),
            P(None, "mp"),
            P(None, None, "mp"),
            P("batch"),
            P("batch"),
            P(None, "batch", "mp"),
        ),
        out_specs=(
            P(None, "batch", None),
            P(None, "batch", "mp"),
            P(None, None, "mp"),
            P(None, "mp"),
            P(None, None, "mp"),
        ),
        check_vma=False,
    )
```
